256 devices in a mesh: dp: 16 (over y_hi, z), blk: 16 (over x, y_lo, core).
Axes of the slice: x: 4, y: 4 (y_hi: 2, y_lo: 2; y = y_hi * 2 + y_lo), z: 8, core: 2. Of those that a mesh axis runs over, the one named last changes fastest.
Arguments:
- images: bfloat16 [131072, 768], P(('dp', 'blk')), may hold values from -0.5412659 to 0.5412659
- captions: bfloat16 [65536, 768], P(('dp', 'blk')), may hold values from -0.5412659 to 0.5412659
- cap_target: int32 [16, 4096], P('dp'), may hold values from 0 to 8191
- cap_count: int32 [16, 256], P('dp'), may hold values from 6 to 16, as said below
Outputs:
- loss_value: float32 [], replicated
- grad_images: float32 [131072, 768], P(('dp', 'blk'))
- grad_captions: float32 [65536, 768], P(('dp', 'blk'))
The draws below stay inside these ranges and needn't reach their ends.
Inputs may be any that keep to these rules, and one draw needn't show every extreme that they name: `cap_count`: entry [g, b * 16 + a] is how many leading slots, of the 16 that the device at dp index a and blk index b sends to data group g, hold a caption; the others are empty. In every draw one data group receives 16 filled slots from every dp index at one blk index.
All inputs are finite; a program needn't handle non-finite values.
Results may differ from the reference program's by a relative error of at most 0.0008.
Values may be sent and summed in bfloat16 or wider, within the bound.
No kernel may reach another device: no remote copies, remote signals or barrier semaphores. Data moves between devices by JAX's collectives and lax.ppermute only.
A program may use at most 128 MiB of HBM per device.

```python
import math
import jax
import jax.numpy as jnp
from jax import lax

D = 768
SLOT = 16
GROUPS = 16
BLOCKS = 16
IMG_GRP = 8192
IMAGES = 131072
GROUP_SLOTS = 4096
CAPTIONS = 65536


def group_factor(group_ids, growth):
    ratio = group_ids.astype(jnp.float32) / (GROUPS - 1)
    return jnp.exp(0.5 * math.log(growth) * ratio)[:, None]


def draw_images(key, part):
    key = jax.random.fold_in(key, 11)
    noise_key, scale_key = jax.random.split(key)
    root_width = math.sqrt(D)
    group_ids = jnp.arange(IMAGES, dtype=jnp.int32) // IMG_GRP
    noise_rows = jnp.clip(jax.random.normal(noise_key, (IMAGES, D)), -5.0, 5.0)
    row_scale = jnp.exp(jax.random.uniform(scale_key, (IMAGES, 1), jnp.float32, math.log(0.3), math.log(1.5)))
    embed_rows = noise_rows * row_scale * group_factor(group_ids, 3.0) / root_width
    return embed_rows.astype(jnp.bfloat16)


def draw_captions(key, part):
    key = jax.random.fold_in(key, 17)
    noise_key, scale_key = jax.random.split(key)
    root_width = math.sqrt(D)
    group_ids = jnp.arange(CAPTIONS, dtype=jnp.int32) // SLOT % GROUPS
    noise_rows = jnp.clip(jax.random.normal(noise_key, (CAPTIONS, D)), -5.0, 5.0)
    row_scale = jnp.exp(jax.random.uniform(scale_key, (CAPTIONS, 1), jnp.float32, math.log(0.3), math.log(1.5)))
    embed_rows = noise_rows * row_scale * group_factor(group_ids, 3.0) / root_width
    return embed_rows.astype(jnp.bfloat16)


def draw_cap_count(key, part):
    key = jax.random.fold_in(key, 23)
    split_keys = jax.random.split(key, 4)
    group_level = jax.random.randint(split_keys[0], (GROUPS, 1), 3 * SLOT // 4, SLOT + 1)
    slot_counts = jax.random.randint(split_keys[1], (GROUPS, BLOCKS * GROUPS), group_level // 2, group_level + 1)
    full_group = jax.random.randint(split_keys[2], (), 0, GROUPS)
    full_block = jax.random.randint(split_keys[3], (), 0, BLOCKS)
    row_pick = jnp.arange(GROUPS, dtype=jnp.int32) == full_group
    column_pick = jnp.arange(BLOCKS * GROUPS, dtype=jnp.int32) // GROUPS == full_block
    slot_counts = jnp.where(row_pick[:, None] & column_pick[None, :], SLOT, slot_counts)
    return slot_counts.astype(jnp.int32)


def place_ends(array, stream_key, smallest, largest):
    dims = array.shape
    spot = [jax.random.randint(jax.random.fold_in(stream_key, axis), (), 0, dims[axis]) for axis in range(len(dims))]
    array = array.at[tuple(spot)].set(smallest)
    longest = dims.index(max(dims))
    spot[longest] = (spot[longest] + 1) % dims[longest]
    return array.at[tuple(spot)].set(largest)


def setup_inputs(seed: int = 0) -> dict:
    streams_of = jax.random.split(jax.random.key(seed), 5)
    return {
        "images": draw_images(jax.random.fold_in(streams_of[4], 71), 0),
        "captions": draw_captions(jax.random.fold_in(streams_of[4], 71), 0),
        "cap_target": place_ends(jax.random.randint(streams_of[2], (GROUPS, GROUP_SLOTS), 0, IMG_GRP), jax.random.fold_in(streams_of[2], 1), 0, IMG_GRP - 1).astype(jnp.int32),
        "cap_count": draw_cap_count(jax.random.fold_in(streams_of[4], 71), 0),
    }


LOGIT_SCALE = 50.0


def group_pass(inputs):
    group_images, group_texts, targets, counts = inputs
    slot_ids = lax.iota(jnp.int32, GROUP_SLOTS)
    live_mask = (slot_ids % SLOT < jnp.repeat(counts, SLOT, total_repeat_length=GROUP_SLOTS)).astype(jnp.float32)
    image_ids = lax.iota(jnp.int32, IMG_GRP)
    hit_mask = jnp.where(targets[None, :] == image_ids[:, None], live_mask[None, :], 0.0)
    scores = jnp.dot(group_images, group_texts.T, preferred_element_type=jnp.float32) * LOGIT_SCALE
    alive_mask = live_mask[None, :] > 0.0
    row_peak = jnp.max(jnp.where(alive_mask, scores, -1.0e30), axis=1)
    row_lse = row_peak + jnp.log(jnp.sum(jnp.where(alive_mask, jnp.exp(scores - row_peak[:, None]), 0.0), axis=1))
    hit_count = jnp.sum(hit_mask, axis=1)
    hit_sum = jnp.sum(hit_mask * scores, axis=1)
    col_peak = jnp.max(scores, axis=0)
    col_lse = col_peak + jnp.log(jnp.sum(jnp.exp(scores - col_peak[None, :]), axis=0))
    live_total = jnp.sum(live_mask)
    hit_floor = jnp.maximum(hit_count, 1.0)
    image_part = jnp.sum(row_lse - hit_sum / hit_floor) / IMG_GRP
    caption_part = (jnp.sum(live_mask * col_lse) - jnp.sum(hit_sum)) / live_total
    group_loss = 0.5 * (image_part + caption_part)
    row_prob = jnp.where(alive_mask, jnp.exp(scores - row_lse[:, None]), 0.0)
    col_prob = jnp.where(alive_mask, jnp.exp(scores - col_lse[None, :]), 0.0)
    balance = IMG_GRP / live_total
    weights = 0.5 * (row_prob - hit_mask / hit_floor[:, None]) + (0.5 * balance) * (col_prob - hit_mask)
    texts_wide = group_texts.astype(jnp.float32)
    images_wide = group_images.astype(jnp.float32)
    image_grad = jnp.dot(weights, texts_wide, precision=lax.Precision.HIGHEST) * LOGIT_SCALE
    text_grad = jnp.dot(weights.T, images_wide, precision=lax.Precision.HIGHEST) * LOGIT_SCALE
    return group_loss, image_grad, text_grad


def reference(images, captions, cap_target, cap_count):
    image_groups = images.reshape(GROUPS, IMG_GRP, D)
    text_groups = captions.reshape(GROUPS, BLOCKS, GROUPS, SLOT, D).transpose(2, 1, 0, 3, 4).reshape(GROUPS, GROUP_SLOTS, D)
    group_losses, image_grads, text_grads = lax.map(group_pass, (image_groups, text_groups, cap_target, cap_count))
    loss_value = jnp.mean(group_losses)
    grad_images = image_grads.reshape(IMAGES, D)
    grad_captions = text_grads.reshape(GROUPS, BLOCKS, GROUPS, SLOT, D).transpose(2, 1, 0, 3, 4).reshape(CAPTIONS, D)
    return (loss_value, grad_images, grad_captions)
```

```python
import math

import jax
import jax.numpy as jnp
from jax import lax
from jax.experimental import pallas as pl
from jax.experimental.pallas import tpu as pltpu
from jax.sharding import PartitionSpec as P

LOGIT_SCALE = 50.0
SCALE_LOG2 = LOGIT_SCALE * math.log2(math.e)
LN2 = math.log(2.0)
VERY_LOW = -1e30
VERY_HIGH = 3e38
VMEM_BYTES = 56 * 1024 * 1024
F32 = jnp.float32
BF16 = jnp.bfloat16

XS, YS, CORES = 4, 2, 2
IMG = 512
CAP = 256
WIDTH = 768
ROWS = 4 * IMG
STEP = 256
STEPS = ROWS // STEP
PER = IMG // STEP


def params(**kw):
    return pltpu.CompilerParams(vmem_limit_bytes=VMEM_BYTES, **kw)


def whole(shape):
    return pl.BlockSpec(shape, lambda *_: (0,) * len(shape))


def image_part(j):
    return pl.BlockSpec((STEP, WIDTH), lambda i: (jnp.clip(i - PER * j, 0, PER - 1), 0))


def move(value, there):
    spots = [(x, y, c) for x in range(XS) for y in range(YS) for c in range(CORES)]
    flat = lambda x, y, c: (x * YS + y) * CORES + c
    return lax.ppermute(value, "blk", [(flat(*s), flat(*there(*s))) for s in spots])


def along_x(value, shift):
    return move(value, lambda x, y, c: ((x + shift) % XS, y, c))


def across(value, q):
    return move(value, lambda x, y, c: (x, y ^ (q >> 1), c ^ (q & 1)))


def row_of(column, lanes=128):
    return jnp.broadcast_to(column, (column.shape[0], lanes)).T[0:1, :]


def column_of(row, lanes=128):
    return jnp.broadcast_to(row, (lanes, row.shape[1])).T


def wide(column, lanes):
    return jnp.concatenate([column] * (lanes // column.shape[1]), axis=1)


def count_kernel(base_ref, balance_ref, targets_ref, out_ref):
    for step in range(STEPS):
        ids = (
            lax.broadcasted_iota(jnp.int32, (STEP, 128), 0)
            + (step % PER) * STEP
            + base_ref[step // PER]
        )

        def add(r, acc):
            return acc + jnp.where(targets_ref[pl.ds(r, 1), :] == ids, 1.0, 0.0)

        hits = lax.fori_loop(0, targets_ref.shape[0], add, jnp.zeros((STEP, 128), F32), unroll=4)
        count = jnp.sum(hits, axis=1, keepdims=True)
        weight = 0.5 / jnp.maximum(count, 1.0) + balance_ref[0]
        out_ref[pl.ds(step * STEP, STEP), :] = jnp.broadcast_to(weight, (STEP, 128))


def hit_weights(base, half_balance, targets):
    smem = pl.BlockSpec(memory_space=pltpu.SMEM)
    return pl.pallas_call(
        count_kernel,
        out_shape=jax.ShapeDtypeStruct((ROWS, 128), F32),
        in_specs=[smem, smem, pl.BlockSpec(memory_space=pltpu.VMEM)],
        out_specs=pl.BlockSpec(memory_space=pltpu.VMEM),
        compiler_params=params(),
        cost_estimate=pl.CostEstimate(flops=20_000_000, bytes_accessed=1 << 20, transcendentals=0),
    )(base, half_balance, targets)


def hit_mask(targets_ref, j, d, step_row, rows):
    ids = lax.broadcasted_iota(jnp.int32, (rows, CAP), 0) + step_row
    return targets_ref[pl.ds(j * 4 + d, 1), :] == ids


def scores_kernel(
    x0, x1, x2, x3, t0, t1, t2, t3, cap_ref, targets_ref, weight_ref,
    s_ref, row_ref, col_ref, xs, cm, cs, hs,
):
    i = pl.program_id(0)
    j = i // PER
    for n, ref in enumerate((x0, x1, x2, x3)):

        @pl.when(j == n)
        def _():
            xs[...] = ref[...]

    @pl.when(i == 0)
    def _():
        cm[...] = jnp.full_like(cm, -VERY_HIGH)
        cs[...] = jnp.zeros_like(cs)
        hs[...] = jnp.zeros_like(hs)

    x = xs[...]
    weight = wide(weight_ref[...], CAP)
    peak = None
    hits = None
    for d, t in enumerate((t0, t1, t2, t3)):
        s = lax.dot_general(x, t[...], (((1,), (1,)), ((), ())), preferred_element_type=F32)
        s = jnp.minimum(s * SCALE_LOG2, cap_ref[d : d + 1, :])
        s_ref[d] = s
        peak = s if peak is None else jnp.maximum(peak, s)
        hit = jnp.where(hit_mask(targets_ref, j, d, (i % PER) * STEP, STEP), s * weight, 0.0)
        hits = hit if hits is None else hits + hit
        old = cm[d : d + 1, :]
        new = jnp.maximum(old, jnp.max(s, axis=0, keepdims=True))
        cm[d : d + 1, :] = new
        cs[d : d + 1, :] = cs[d : d + 1, :] * jnp.exp2(old - new) + jnp.sum(
            jnp.exp2(s - new), axis=0, keepdims=True
        )
    hs[0:1, :] = hs[0:1, :] + jnp.sum(hits, axis=0, keepdims=True)
    peak = jnp.max(peak, axis=1, keepdims=True)
    mass = None
    for d in range(4):
        e = jnp.exp2(s_ref[d] - peak)
        mass = e if mass is None else mass + e
    mass = jnp.sum(mass, axis=1, keepdims=True)
    row_ref[pl.ds(i, 1), :] = row_of(peak + jnp.log2(mass))

    @pl.when(i == STEPS - 1)
    def _():
        col_ref[0:4, :] = cm[0:4, :] + jnp.log2(cs[0:4, :])
        col_ref[4:8, :] = jnp.concatenate([hs[0:1, :], jnp.zeros((3, CAP), F32)], axis=0)


def scores(images, texts, cap, targets, weight):
    return pl.pallas_call(
        scores_kernel,
        grid=(STEPS,),
        out_shape=(
            jax.ShapeDtypeStruct((4, ROWS, CAP), F32),
            jax.ShapeDtypeStruct((STEPS, STEP), F32),
            jax.ShapeDtypeStruct((8, CAP), F32),
        ),
        in_specs=[image_part(j) for j in range(4)]
        + [whole((CAP, WIDTH))] * 4
        + [whole((8, CAP)), whole((16, CAP)), pl.BlockSpec((STEP, 128), lambda i: (i, 0))],
        out_specs=(
            pl.BlockSpec((4, STEP, CAP), lambda i: (0, i, 0)),
            whole((STEPS, STEP)),
            whole((8, CAP)),
        ),
        scratch_shapes=[
            pltpu.VMEM((STEP, WIDTH), BF16),
            pltpu.VMEM((8, CAP), F32),
            pltpu.VMEM((8, CAP), F32),
            pltpu.VMEM((8, CAP), F32),
        ],
        compiler_params=params(),
        cost_estimate=pl.CostEstimate(
            flops=2 * ROWS * 4 * CAP * WIDTH, bytes_accessed=14 << 20, transcendentals=4 << 20
        ),
    )(*images, *texts, cap, targets, weight)


def combine(parts):
    peak = parts[0]
    for p in parts[1:]:
        peak = jnp.maximum(peak, p)
    mass = None
    for p in parts:
        e = jnp.exp2(p - peak)
        mass = e if mass is None else mass + e
    return peak + jnp.log2(mass)


def pick(ref, order):
    return jnp.concatenate([ref[o : o + 1, :] for o in order], axis=0)


def two_terms(w):
    high = w.astype(BF16)
    return high, (w - high.astype(F32)).astype(BF16)


def text_kernel(
    scal_ref, s_ref, x0, x1, x2, x3, row0, row1, row2, row3, col0, col1, col2, col3,
    cap_ref, targets_ref, weight_ref,
    o0, o1, o2, o3, r_ref, c_ref, loss_ref, hi, lo,
):
    d = pl.program_id(0)

    @pl.when(d == 0)
    def _():
        rows = [
            pick(ref, [((i // PER) ^ q) * PER + i % PER for i in range(STEPS)])
            for q, ref in enumerate((row0, row1, row2, row3))
        ]
        r = combine(rows)
        cols = [
            pick(ref, [(n + e) % 4 for n in range(4)])
            for e, ref in enumerate((col0, col1, col2, col3))
        ]
        alive = cap_ref[0:4, :] > 0.0
        c = jnp.where(alive, combine(cols), 0.0)
        share = (
            jnp.sum(r) * scal_ref[1] + jnp.sum(c) * scal_ref[2] - jnp.sum(col0[4:5, :]) * scal_ref[3]
        )
        loss_ref[...] = jnp.full_like(loss_ref, share)
        c_ref[0:4, :] = jnp.where(alive, c - scal_ref[0], 0.0)
        c_ref[4:8, :] = jnp.zeros((4, CAP), F32)
        for i in range(STEPS):
            r_ref[i * STEP : (i + 1) * STEP, :] = column_of(r[i : i + 1, :] + 1.0)

    col = c_ref[pl.ds(d, 1), :]
    acc = None
    for j, x in enumerate((x0, x1, x2, x3)):
        for h in range(PER):
            at = slice((j * PER + h) * STEP, (j * PER + h + 1) * STEP)
            s = s_ref[0, at, :]
            w = jnp.exp2(s - wide(r_ref[at, :], CAP)) + jnp.exp2(s - col)
            w = w - jnp.where(
                hit_mask(targets_ref, j, d, h * STEP, STEP), wide(weight_ref[at, :], CAP), 0.0
            )
            hi[at, :], lo[at, :] = two_terms(w)
        at = slice(j * IMG, (j + 1) * IMG)
        for part in (hi, lo):
            term = lax.dot_general(
                part[at, :], x[...], (((0,), (0,)), ((), ())), preferred_element_type=F32
            )
            acc = term if acc is None else acc + term
    for n, o in enumerate((o0, o1, o2, o3)):

        @pl.when(d == n)
        def _():
            o[...] = acc


def text_terms(scal, s, images, rows, cols, cap, targets, weight):
    small = whole((8, CAP))
    return pl.pallas_call(
        text_kernel,
        grid=(4,),
        out_shape=(jax.ShapeDtypeStruct((CAP, WIDTH), F32),) * 4
        + (
            jax.ShapeDtypeStruct((ROWS, 128), F32),
            jax.ShapeDtypeStruct((8, CAP), F32),
            jax.ShapeDtypeStruct((8, 128), F32),
        ),
        in_specs=[
            pl.BlockSpec(memory_space=pltpu.SMEM),
            pl.BlockSpec((1, ROWS, CAP), lambda d: (d, 0, 0)),
        ]
        + [whole((IMG, WIDTH))] * 4
        + [small] * 9
        + [whole((16, CAP)), whole((ROWS, 128))],
        out_specs=(whole((CAP, WIDTH)),) * 4
        + (whole((ROWS, 128)), whole((8, CAP)), whole((8, 128))),
        scratch_shapes=[pltpu.VMEM((ROWS, CAP), BF16), pltpu.VMEM((ROWS, CAP), BF16)],
        compiler_params=params(),
        cost_estimate=pl.CostEstimate(
            flops=4 * ROWS * 4 * CAP * WIDTH, bytes_accessed=16 << 20, transcendentals=4 << 20
        ),
    )(scal, s, *images, *rows, *cols, cap, targets, weight)


def image_kernel(
    s_ref, r_ref, c_ref, t0, t1, t2, t3, targets_ref, weight_ref, y0, y1, y2, y3
):
    i = pl.program_id(0)
    j = i // PER
    acc = None
    r = wide(r_ref[...], CAP)
    weight = wide(weight_ref[...], CAP)
    for d, t in enumerate((t0, t1, t2, t3)):
        s = s_ref[d]
        w = jnp.exp2(s - r) + jnp.exp2(s - c_ref[d : d + 1, :])
        w = w - jnp.where(hit_mask(targets_ref, j, d, (i % PER) * STEP, STEP), weight, 0.0)
        for part in two_terms(w):
            term = jnp.dot(part, t[...], preferred_element_type=F32)
            acc = term if acc is None else acc + term
    for n, y in enumerate((y0, y1, y2, y3)):

        @pl.when(j == n)
        def _():
            y[...] = acc


def image_terms(s, r, c, texts, targets, weight):
    run = pl.BlockSpec((STEP, 128), lambda i: (i, 0))
    return pl.pallas_call(
        image_kernel,
        grid=(STEPS,),
        out_shape=(jax.ShapeDtypeStruct((IMG, WIDTH), F32),) * 4,
        in_specs=[pl.BlockSpec((4, STEP, CAP), lambda i: (0, i, 0)), run, whole((8, CAP))]
        + [whole((CAP, WIDTH))] * 4
        + [whole((16, CAP)), run],
        out_specs=tuple(image_part(j) for j in range(4)),
        compiler_params=params(),
        cost_estimate=pl.CostEstimate(
            flops=4 * ROWS * 4 * CAP * WIDTH, bytes_accessed=16 << 20, transcendentals=4 << 20
        ),
    )(s, r, c, *texts, targets, weight)


def total(value):
    value = sum((across(value, q) for q in (1, 2, 3)), value)
    value = sum((along_x(value, e) for e in (1, 2, 3)), value)
    n = lax.axis_size("dp")
    for unit in (1, 4):
        shifts = [(lambda a, e=e: a // (4 * unit) * (4 * unit) + (a + e * unit) % (4 * unit)) for e in (1, 2, 3)]
        value = sum((lax.ppermute(value, "dp", [(a, to(a)) for a in range(n)]) for to in shifts), value)
    return value


def shards(images, captions, cap_target, cap_count):
    groups = lax.axis_size("dp")
    blocks = lax.axis_size("blk")
    slots = cap_target.shape[1]
    slot_size = slots // (groups * blocks)
    me = lax.axis_index("blk")
    my_x, my_yc = me // (YS * CORES), me % (YS * CORES)

    image1 = across(images, 1)
    image2 = across(images, 2)
    received = lax.all_to_all(captions, "dp", split_axis=0, concat_axis=0, tiled=True)
    image3 = across(image2, 1)
    parts = (images, image1, image2, image3)
    texts = (received,) + tuple(along_x(received, -d) for d in (1, 2, 3))

    alive = lax.iota(jnp.int32, slots) % slot_size < jnp.repeat(cap_count[0], slot_size)
    targets = jnp.where(alive, cap_target[0], -1)
    caps = jnp.where(alive, VERY_HIGH, VERY_LOW).astype(F32)
    live = jnp.sum(cap_count[0]).astype(F32)
    group_images = float(IMG * blocks)
    half_balance = 0.5 * group_images / live
    order = [(my_x + d) % XS * (YS * CORES) + my_yc for d in range(4)]
    take = lambda a: jnp.stack([lax.dynamic_index_in_dim(a.reshape(blocks, CAP), o, 0, False) for o in order])
    base = jnp.stack([(my_x * 4 + (my_yc ^ q)) * IMG for q in range(4)]).astype(jnp.int32)
    my_targets = (take(targets)[None] - base[:, None, None]).reshape(16, CAP)
    my_caps = jnp.concatenate([take(caps), jnp.zeros((4, CAP), F32)], axis=0)
    weight = hit_weights(base, half_balance[None], targets.reshape(-1, 128))

    s, row, col = scores(parts, texts, my_caps, my_targets, weight)
    rows = (row,) + tuple(across(row, q) for q in (1, 2, 3))
    cols = (col,) + tuple(along_x(col, e) for e in (1, 2, 3))
    scal = jnp.stack(
        [
            jnp.log2(half_balance),
            jnp.float32(LN2 * 0.5 / group_images / 4 / groups),
            LN2 * 0.5 / live / 4 / groups,
            jnp.float32(LN2 / group_images / groups),
        ]
    )
    *terms, r, c, loss = text_terms(scal, s, parts, rows, cols, my_caps, my_targets, weight)
    sent = [along_x(terms[d], d) for d in (1, 2, 3)]
    y0, y1, y2, y3 = image_terms(s, r, c, texts, my_targets, weight)
    text_grad = (terms[0] + sent[0] + sent[1] + sent[2]) * LOGIT_SCALE
    grad_captions = lax.all_to_all(text_grad, "dp", split_axis=0, concat_axis=0, tiled=True)
    a3 = across(y3, 1)
    a1 = across(y1, 1)
    b = across(y2 + a3, 2)
    image_grad = (y0 + a1 + b) * LOGIT_SCALE
    loss_value = total(loss)[0, 0]
    return loss_value, image_grad, grad_captions


def solution(mesh):
    return jax.shard_map(
        shards,
        mesh=mesh,
        in_specs=(P(("dp", "blk"), None), P(("dp", "blk"), None), P("dp", None), P("dp", None)),
        out_specs=(P(), P(("dp", "blk"), None), P(("dp", "blk"), None)),
        check_vma=False,
    )
```

```python
import functools
import math

import jax
import jax.numpy as jnp
from jax import lax
from jax.experimental import pallas as pl
from jax.experimental.pallas import tpu as pltpu
from jax.sharding import PartitionSpec as P

LOGIT_SCALE = 50.0
SCALE_LOG2 = LOGIT_SCALE * math.log2(math.e)
LN2 = math.log(2.0)
SEND_SCALE = 16.0
VERY_LOW = -1e30
VERY_HIGH = 3e38
VMEM_BYTES = 18 * 1024 * 1024
F32 = jnp.float32
BF16 = jnp.bfloat16

XS, YS, CORES = 4, 2, 2
IMG = 512
CAP = 256
WIDTH = 768
ROWS = 4 * IMG
STEP = 256
STEPS = ROWS // STEP
PER = IMG // STEP


def call(kernel, out, args, smem=0, scratch=(), flops=0):
    vmem = pl.BlockSpec(memory_space=pltpu.VMEM)
    scalars = [pl.BlockSpec(memory_space=pltpu.SMEM)] * smem
    return pl.pallas_call(
        kernel,
        out_shape=tuple(jax.ShapeDtypeStruct(*o) for o in out),
        in_specs=scalars + [vmem] * (len(args) - smem),
        out_specs=(vmem,) * len(out),
        scratch_shapes=list(scratch),
        compiler_params=pltpu.CompilerParams(vmem_limit_bytes=VMEM_BYTES),
        cost_estimate=pl.CostEstimate(flops=flops, bytes_accessed=1 << 16, transcendentals=0),
    )(*args)


def move(value, there):
    spots = [(x, y, c) for x in range(XS) for y in range(YS) for c in range(CORES)]
    flat = lambda x, y, c: (x * YS + y) * CORES + c
    return lax.ppermute(value, "blk", [(flat(*s), flat(*there(*s))) for s in spots])


def along_x(value, shift):
    return move(value, lambda x, y, c: ((x + shift) % XS, y, c))


def across(value, q):
    return move(value, lambda x, y, c: (x, y ^ (q >> 1), c ^ (q & 1)))


def row_of(column, lanes=128):
    return jnp.broadcast_to(column, (column.shape[0], lanes)).T[0:1, :]


def column_of(row, lanes=128):
    return jnp.broadcast_to(row, (lanes, row.shape[1])).T


def wide(column, lanes):
    return jnp.concatenate([column] * (lanes // column.shape[1]), axis=1)


def count_kernel(base_ref, balance_ref, targets_ref, out_ref):
    for step in range(STEPS):
        ids = (
            lax.broadcasted_iota(jnp.int32, (STEP, 128), 0)
            + (step % PER) * STEP
            + base_ref[step // PER]
        )

        def add(r, acc):
            return acc + jnp.where(targets_ref[pl.ds(r, 1), :] == ids, 1.0, 0.0)

        hits = lax.fori_loop(0, targets_ref.shape[0], add, jnp.zeros((STEP, 128), F32), unroll=4)
        count = jnp.sum(hits, axis=1, keepdims=True)
        weight = 0.5 / jnp.maximum(count, 1.0) + balance_ref[0]
        out_ref[pl.ds(step * STEP, STEP), :] = jnp.broadcast_to(weight, (STEP, 128))


def hit_weights(base, half_balance, targets):
    return call(
        count_kernel, [((ROWS, 128), F32)], (base, half_balance, targets), smem=2, flops=1 << 20
    )[0]


def hit_mask(targets_ref, j, d, first, rows):
    ids = lax.broadcasted_iota(jnp.int32, (rows, CAP), 0) + first
    return targets_ref[j * 4 + d : j * 4 + d + 1, :] == ids


def scores_kernel(d, n_others, *refs):
    (x0, x1, x2, x3, t_ref, cap_ref, targets_ref, weight_ref), refs = refs[:8], refs[8:]
    others, (s_ref, row_ref, col_ref, cm, cs) = refs[: 2 * n_others], refs[2 * n_others :]
    cap = cap_ref[d : d + 1, :]
    hits = None
    for i in range(STEPS):
        at = slice(i * STEP, (i + 1) * STEP)
        x = (x0, x1, x2, x3)[i // PER][(i % PER) * STEP : (i % PER + 1) * STEP, :]
        s = lax.dot_general(x, t_ref[...], (((1,), (1,)), ((), ())), preferred_element_type=F32)
        s = jnp.minimum(s * SCALE_LOG2, cap)
        s_ref[at, :] = s
        top = jnp.max(s, axis=0, keepdims=True)
        cm[i : i + 1, :] = top
        cs[i : i + 1, :] = jnp.sum(jnp.exp2(s - top), axis=0, keepdims=True)
        hit = hit_mask(targets_ref, i // PER, d, (i % PER) * STEP, STEP)
        score = jnp.where(hit, s * wide(weight_ref[at, :], CAP), 0.0)
        score = jnp.sum(score, axis=0, keepdims=True)
        hits = score if hits is None else hits + score
        peak = jnp.max(s, axis=1, keepdims=True)
        mass = jnp.sum(jnp.exp2(s - peak), axis=1, keepdims=True)
        row_ref[i : i + 1, :] = row_of(peak + jnp.log2(mass))
    top = jnp.max(cm[...], axis=0, keepdims=True)
    mass = jnp.sum(cs[...] * jnp.exp2(cm[...] - top), axis=0, keepdims=True)
    col_ref[...] = jnp.zeros_like(col_ref)
    col_ref[d : d + 1, :] = top + jnp.log2(mass)
    col_ref[4 + d : 5 + d, :] = hits
    if others:
        row_ref[...] = combine([row_ref[...]] + [o[...] for o in others[0::2]])
        col_ref[...] = sum((o[...] for o in others[1::2]), col_ref[...])


def scores(d, images, text, cap, targets, weight, others):
    return call(
        functools.partial(scores_kernel, d, len(others) // 2),
        [((ROWS, CAP), F32), ((STEPS, STEP), F32), ((8, CAP), F32)],
        (*images, text, cap, targets, weight, *others),
        scratch=[pltpu.VMEM((STEPS, CAP), F32)] * 2,
        flops=1 << 20,
    )


def combine(parts):
    peak = parts[0]
    for p in parts[1:]:
        peak = jnp.maximum(peak, p)
    mass = None
    for p in parts:
        e = jnp.exp2(p - peak)
        mass = e if mass is None else mass + e
    return peak + jnp.log2(mass)


def pick(ref, order):
    return jnp.concatenate([ref[o : o + 1, :] for o in order], axis=0)


def two_terms(w):
    high = w.astype(BF16)
    return high, (w - high.astype(F32)).astype(BF16)


def stats_kernel(
    scal_ref, row0, row1, row2, row3, col0, col1, col2, col3, cap_ref, r_ref, c_ref, sum_ref
):
    rows = [
        pick(ref, [((i // PER) ^ q) * PER + i % PER for i in range(STEPS)])
        for q, ref in enumerate((row0, row1, row2, row3))
    ]
    r = combine(rows)
    cols = [
        pick(ref, [(n + e) % 4 for n in range(4)])
        for e, ref in enumerate((col0, col1, col2, col3))
    ]
    alive = cap_ref[0:4, :] > 0.0
    c = jnp.where(alive, combine(cols), 0.0)
    c_ref[0:4, :] = jnp.where(alive, c - scal_ref[0], 0.0)
    c_ref[4:8, :] = jnp.zeros((4, CAP), F32)
    for i in range(STEPS):
        r_ref[i * STEP : (i + 1) * STEP, :] = column_of(r[i : i + 1, :] + 1.0)
    share = jnp.sum(r, axis=0, keepdims=True) * scal_ref[1]
    share = share + jnp.sum(c, axis=0, keepdims=True) * scal_ref[2]
    share = share - jnp.sum(col0[4:8, :], axis=0, keepdims=True) * scal_ref[3]
    sum_ref[...] = jnp.broadcast_to(share[:, 0:128] + share[:, 128:256], (8, 128))


def statistics(scal, rows, cols, cap):
    return call(
        stats_kernel,
        [((ROWS, 128), F32), ((8, CAP), F32), ((8, 128), F32)],
        (scal, *rows, *cols, cap),
        smem=1,
        flops=1 << 20,
    )


def text_kernel(d, s_ref, x0, x1, x2, x3, r_ref, c_ref, targets_ref, weight_ref, o_ref):
    acc = None
    for j, x in enumerate((x0, x1, x2, x3)):
        at = slice(j * IMG, (j + 1) * IMG)
        s = s_ref[at, :]
        w = jnp.exp2(s - wide(r_ref[at, :], CAP)) + jnp.exp2(s - c_ref[d : d + 1, :])
        hit = hit_mask(targets_ref, j, d, 0, IMG)
        w = w - jnp.where(hit, wide(weight_ref[at, :], CAP), 0.0)
        for part in two_terms(w):
            term = lax.dot_general(part, x[...], (((0,), (0,)), ((), ())), preferred_element_type=F32)
            acc = term if acc is None else acc + term
    o_ref[...] = acc


def text_terms(d, s, images, r, c, targets, weight):
    return call(
        functools.partial(text_kernel, d),
        [((CAP, WIDTH), F32)],
        (s, *images, r, c, targets, weight),
        flops=1 << 20,
    )[0]


def image_kernel(
    js, s0, s1, s2, s3, t0, t1, t2, t3, r_ref, c_ref, targets_ref, weight_ref, *outs
):
    for j, y in zip(js, outs):
        at = slice(j * IMG, (j + 1) * IMG)
        acc = None
        r = wide(r_ref[at, :], CAP)
        weight = wide(weight_ref[at, :], CAP)
        for d, (s_ref, t) in enumerate(((s0, t0), (s1, t1), (s2, t2), (s3, t3))):
            s = s_ref[at, :]
            w = jnp.exp2(s - r) + jnp.exp2(s - c_ref[d : d + 1, :])
            w = w - jnp.where(hit_mask(targets_ref, j, d, 0, IMG), weight, 0.0)
            for part in two_terms(w):
                term = jnp.dot(part, t[...], preferred_element_type=F32)
                acc = term if acc is None else acc + term
        y[...] = acc


def image_terms(js, s, texts, r, c, targets, weight):
    return call(
        functools.partial(image_kernel, js),
        [((IMG, WIDTH), F32)] * len(js),
        (*s, *texts, r, c, targets, weight),
        flops=1 << 20,
    )


def total_over(value, moves):
    return sum((m(value) for m in moves), value)


def dp_moves():
    n = lax.axis_size("dp")
    for unit in (1, 4):
        size = 4 * unit
        yield [[(a, a // size * size + (a + e * unit) % size) for a in range(n)] for e in (1, 2, 3)]


def after(*values):
    return lax.optimization_barrier(values)


def pack(value):
    return (value * SEND_SCALE).astype(jnp.float16)


def unpack(value):
    return value.astype(F32) * (1.0 / SEND_SCALE)


def shards(images, captions, cap_target, cap_count):
    groups = lax.axis_size("dp")
    blocks = lax.axis_size("blk")
    slots = cap_target.shape[1]
    slot_size = slots // (groups * blocks)
    me = lax.axis_index("blk")
    my_x, my_yc = me // (YS * CORES), me % (YS * CORES)

    image1 = across(images, 1)
    image2 = across(images, 2)
    received = lax.all_to_all(captions, "dp", split_axis=0, concat_axis=0, tiled=True)
    image3 = across(image2, 1)
    parts = (images, image1, image2, image3)
    texts = (received,) + tuple(along_x(received, -d) for d in (1, 2, 3))

    alive = lax.iota(jnp.int32, slots) % slot_size < jnp.repeat(cap_count[0], slot_size)
    targets = jnp.where(alive, cap_target[0], -1)
    caps = jnp.where(alive, VERY_HIGH, VERY_LOW).astype(F32)
    live = jnp.sum(cap_count[0]).astype(F32)
    group_images = float(IMG * blocks)
    half_balance = 0.5 * group_images / live
    order = [(my_x + d) % XS * (YS * CORES) + my_yc for d in range(4)]
    take = lambda a: jnp.stack([lax.dynamic_index_in_dim(a.reshape(blocks, CAP), o, 0, False) for o in order])
    base = jnp.stack([(my_x * 4 + (my_yc ^ q)) * IMG for q in range(4)]).astype(jnp.int32)
    my_targets = (take(targets)[None] - base[:, None, None]).reshape(16, CAP)
    my_caps = jnp.concatenate([take(caps), jnp.zeros((4, CAP), F32)], axis=0)
    weight = hit_weights(base, half_balance[None], targets.reshape(-1, 128))

    s, found = [None] * 4, []
    for d in (0, 1, 3, 2):
        s[d], row, col = scores(
            d, parts, texts[d], my_caps, my_targets, weight, found if d == 2 else []
        )
        found += [row, col]
    rows = (row,) + tuple(across(row, q) for q in (1, 2, 3))
    cols = (col,) + tuple(along_x(col, e) for e in (1, 2, 3))
    scal = jnp.stack(
        [
            jnp.log2(half_balance),
            jnp.float32(LN2 * 0.5 / group_images / 4 / groups),
            LN2 * 0.5 / live / 4 / groups,
            jnp.float32(LN2 / group_images / groups),
        ]
    )
    r, c, loss = statistics(scal, rows, cols, my_caps)
    sent = [None] * 4
    loss = total_over(loss, [lambda v, q=q: across(v, q) for q in (1, 2, 3)])
    for d in (2, 1, 3):
        part = pack(text_terms(d, s[d], parts, r, c, my_targets, weight))
        sent[d] = along_x(part, d)
        r, *_ = after(r, part, *((loss,) if d == 1 else ()))
    loss = total_over(loss, [lambda v, e=e: along_x(v, e) for e in (1, 2, 3)])
    y3, y1 = image_terms((3, 1), s, texts, r, c, my_targets, weight)
    own = text_terms(0, s[0], parts, r, c, my_targets, weight)
    y2, y0 = image_terms((2, 0), s, texts, r, c, my_targets, weight)
    y3, y1, y2, y0, own, loss, *sent = after(y3, y1, y2, y0, own, loss, *sent[1:])
    a3, a1 = across(y3, 1), across(y1, 1)
    one, two = dp_moves()
    loss = total_over(loss, [lambda v, m=m: lax.ppermute(v, "dp", m) for m in one])
    b = across(pack(y2 + a3), 2)
    text_grad = pack(own + unpack(sent[0]) + unpack(sent[1]) + unpack(sent[2]))
    text_grad, loss = after(text_grad, loss)
    text_grad = lax.all_to_all(text_grad, "dp", split_axis=0, concat_axis=0, tiled=True)
    grad_captions = unpack(text_grad) * LOGIT_SCALE
    loss = total_over(loss, [lambda v, m=m: lax.ppermute(v, "dp", m) for m in two])
    image_grad = (y0 + a1 + unpack(b)) * LOGIT_SCALE
    loss_value = jnp.sum(loss[0])
    return loss_value, image_grad, grad_captions


def solution(mesh):
    return jax.shard_map(
        shards,
        mesh=mesh,
        in_specs=(P(("dp", "blk"), None), P(("dp", "blk"), None), P("dp", None), P("dp", None)),
        out_specs=(P(), P(("dp", "blk"), None), P(("dp", "blk"), None)),
        check_vma=False,
    )
```

```python
import functools
import math

import jax
import jax.numpy as jnp
from jax import lax
from jax.experimental import pallas as pl
from jax.experimental.pallas import tpu as pltpu
from jax.sharding import PartitionSpec as P

LOGIT_SCALE = 50.0
SCALE_LOG2 = LOGIT_SCALE * math.log2(math.e)
LN2 = math.log(2.0)
SEND_SCALE = 16.0
VERY_LOW = -1e30
VERY_HIGH = 3e38
VMEM_BYTES = 20 * 1024 * 1024
F32 = jnp.float32
BF16 = jnp.bfloat16

XS, YS, CORES = 4, 2, 2
IMG = 512
CAP = 256
WIDTH = 768
ROWS = 4 * IMG
SLOT = 16
HALF = 64
CHUNK = 32


def call(kernel, out, args, smem=0, scratch=()):
    vmem = pl.BlockSpec(memory_space=pltpu.VMEM)
    scalars = [pl.BlockSpec(memory_space=pltpu.SMEM)] * smem
    return pl.pallas_call(
        kernel,
        out_shape=tuple(jax.ShapeDtypeStruct(*o) for o in out),
        in_specs=scalars + [vmem] * (len(args) - smem),
        out_specs=(vmem,) * len(out),
        scratch_shapes=list(scratch),
        compiler_params=pltpu.CompilerParams(vmem_limit_bytes=VMEM_BYTES),
        cost_estimate=pl.CostEstimate(flops=1 << 20, bytes_accessed=1 << 16, transcendentals=0),
    )(*args)


def move(value, there):
    spots = [(x, y, c) for x in range(XS) for y in range(YS) for c in range(CORES)]
    flat = lambda x, y, c: (x * YS + y) * CORES + c
    return lax.ppermute(value, "blk", [(flat(*s), flat(*there(*s))) for s in spots])


def along_x(value, shift):
    return move(value, lambda x, y, c: ((x + shift) % XS, y, c))


def across(value, q):
    return move(value, lambda x, y, c: (x, y ^ (q >> 1), c ^ (q & 1)))


def row_of(column, lanes=128):
    return jnp.broadcast_to(column, (column.shape[0], lanes)).T[0:1, :]


def column_of(row, lanes=128):
    return jnp.broadcast_to(row, (lanes, row.shape[1])).T


def wide(column, lanes):
    return jnp.concatenate([column] * (lanes // column.shape[1]), axis=1)


def log_sum(parts):
    peak = functools.reduce(jnp.maximum, parts)
    return peak + jnp.log2(sum(jnp.exp2(p - peak) for p in parts))


def setup_kernel(base_ref, order_ref, balance_ref, targets_ref, weight_ref, column_ref, mine_ref):
    mine_ref[...] = jnp.zeros_like(mine_ref)
    for d in range(4):
        row = targets_ref[pl.ds(order_ref[d], 1), :]
        mine_ref[d : d + 1, :] = row
        column_ref[d * CAP : (d + 1) * CAP, :] = column_of(row)
    weight_ref[...] = jnp.zeros_like(weight_ref)
    step = 256
    for i in range(ROWS // step):
        j, at = i * step // IMG, i * step % IMG
        ids = lax.broadcasted_iota(jnp.int32, (step, 128), 0).astype(F32) + (base_ref[j] + at).astype(F32)

        def add(b, acc):
            row = targets_ref[pl.ds(b, 1), :]
            for h in range(CAP // 128):
                acc = acc + jnp.where(row[:, h * 128 : (h + 1) * 128] == ids, 1.0, 0.0)
            return acc

        hits = lax.fori_loop(0, targets_ref.shape[0], add, jnp.zeros((step, 128), F32), unroll=2)
        count = jnp.sum(hits, axis=1, keepdims=True)
        weight_ref[j : j + 1, at : at + step] = row_of(0.5 / jnp.maximum(count, 1.0) + balance_ref[0])


def setup(base, order, balance, targets):
    return call(
        setup_kernel,
        [((8, IMG), F32), ((4 * CAP, 128), F32), ((8, CAP), F32)],
        (base, order, balance, targets),
        smem=3,
    )


def join_kernel(x0, x1, x2, x3, column_in, weight_in, x_ref, column_ref, weight_ref):
    for j, x in enumerate((x0, x1, x2, x3)):
        x_ref[j * IMG : (j + 1) * IMG, :] = x[...]
    column_ref[...] = column_in[...]
    weight_ref[...] = weight_in[...]


def join(images, column, weight):
    return call(
        join_kernel,
        [((ROWS, WIDTH), BF16), ((4 * CAP, 128), F32), ((8, IMG), F32)],
        (*images, column, weight),
    )


def tiles(s):
    return [s[:, n : n + 128] for n in range(0, s.shape[1], 128)]


def fold(op, s):
    return functools.reduce(op, [s[n : n + 8, :] for n in range(0, s.shape[0], 8)])


def scores_kernel(d, n_others, base_ref, *refs):
    (x_ref, t_ref, column_ref, weight_ref), refs = refs[:4], refs[4:]
    others, refs = refs[: 2 * n_others], refs[2 * n_others :]
    s_ref, img_ref, cap_ref, dots0, dots1, peak, mass = refs
    img_ref[...] = jnp.zeros_like(img_ref)
    hits = jnp.zeros((8, IMG), F32)
    for j in range(4):
        cols = slice(j * IMG, (j + 1) * IMG)
        dots = (dots0, dots1)[j % 2]
        dots[...] = lax.dot_general(
            t_ref[...], x_ref[cols, :], (((1,), (1,)), ((), ())), preferred_element_type=F32
        )
        ids = (lax.broadcasted_iota(jnp.int32, (1, IMG), 1) + base_ref[j]).astype(F32)
        weight = weight_ref[j : j + 1, :]
        top = jnp.full((8, IMG), -VERY_HIGH, F32)
        for n in range(0, CAP, CHUNK):
            at = slice(n, n + CHUNK)
            target = column_ref[d * CAP + n : d * CAP + n + CHUNK, :]
            limit = wide(jnp.where(target < 0.0, VERY_LOW, VERY_HIGH), IMG)
            s = jnp.minimum(dots[at, :] * SCALE_LOG2, limit)
            s_ref[at, cols] = s
            top = jnp.maximum(top, fold(jnp.maximum, s))
            hits = hits + fold(jnp.add, jnp.where(wide(target, IMG) == ids, s * weight, 0.0))
            new = functools.reduce(jnp.maximum, tiles(s))
            if j:
                old = peak[at, :]
                new = jnp.maximum(new, old)
                mass[at, :] = mass[at, :] * jnp.exp2(old - new)
            peak[at, :] = new
        top = jnp.max(top, axis=0, keepdims=True)
        total = jnp.zeros((8, IMG), F32)
        for n in range(0, CAP, CHUNK):
            at = slice(n, n + CHUNK)
            s = s_ref[at, cols]
            total = total + fold(jnp.add, jnp.exp2(s - top))
            add = sum(jnp.exp2(p - peak[at, :]) for p in tiles(s))
            mass[at, :] = mass[at, :] + add if j else add
        img_ref[j : j + 1, :] = top + jnp.log2(jnp.sum(total, axis=0, keepdims=True))
    img_ref[4:5, :] = jnp.sum(hits, axis=0, keepdims=True)
    top = jnp.max(peak[...], axis=1, keepdims=True)
    total = jnp.sum(mass[...] * jnp.exp2(peak[...] - top), axis=1, keepdims=True)
    cap_ref[...] = jnp.zeros_like(cap_ref)
    cap_ref[d : d + 1, :] = row_of(top + jnp.log2(total))
    if others:
        img, cap = others[0::2], others[1::2]
        img_ref[0:4, :] = log_sum([img_ref[0:4, :]] + [o[0:4, :] for o in img])
        img_ref[4:5, :] = sum((o[4:5, :] for o in img), img_ref[4:5, :])
        cap_ref[...] = sum((o[...] for o in cap), cap_ref[...])


def scores(d, base, images, text, column, weight, others):
    return call(
        functools.partial(scores_kernel, d, len(others) // 2),
        [((CAP, ROWS), F32), ((8, IMG), F32), ((8, CAP), F32)],
        (base, images, text, column, weight, *others),
        smem=1,
        scratch=[pltpu.VMEM((CAP, IMG), F32)] * 2 + [pltpu.VMEM((CAP, 128), F32)] * 2,
    )


def stats_kernel(
    scal_ref, img0, img1, img2, img3, cap0, cap1, cap2, cap3, mine_ref, r_ref, c_ref, a_ref, b_ref
):
    pick = lambda ref, order: jnp.concatenate([ref[o : o + 1, :] for o in order], axis=0)
    imgs, caps = (img0, img1, img2, img3), (cap0, cap1, cap2, cap3)
    r = log_sum([pick(ref, [j ^ q for j in range(4)]) for q, ref in enumerate(imgs)])
    r_ref[0:4, :] = r + 1.0
    r_ref[4:8, :] = jnp.zeros((4, IMG), F32)
    alive = mine_ref[0:4, :] >= 0.0
    c = log_sum([pick(ref, [(d + e) % 4 for d in range(4)]) for e, ref in enumerate(caps)])
    c = jnp.where(alive, c, 0.0)
    moved = jnp.where(alive, c - jnp.log2(jnp.full_like(c, scal_ref[0])), 0.0)
    for d in range(4):
        c_ref[d * CAP : (d + 1) * CAP, :] = column_of(moved[d : d + 1, :])
    hits = sum(ref[4:5, :] for ref in imgs)
    a = jnp.sum(r) * scal_ref[1] - jnp.sum(hits) * scal_ref[3]
    a = jnp.full((8, WIDTH), a, F32)
    high = a.astype(BF16).astype(F32)
    a_ref[0:8, :] = high
    a_ref[8:16, :] = a - high
    b_ref[...] = jnp.full((8, 128), jnp.sum(c) * scal_ref[2], F32)


def statistics(scal, imgs, caps, mine):
    return call(
        stats_kernel,
        [((8, IMG), F32), ((4 * CAP, 128), F32), ((16, WIDTH), F32), ((8, 128), F32)],
        (scal, *imgs, *caps, mine),
        smem=1,
    )


def split_weights(d, j, base_ref, s_ref, r_ref, c_ref, column_ref, weight_ref, high_ref, low_ref):
    ids = (lax.broadcasted_iota(jnp.int32, (1, IMG), 1) + base_ref[j]).astype(F32)
    r = r_ref[j : j + 1, :]
    weight = weight_ref[j : j + 1, :]
    for n in range(0, CAP, CHUNK):
        rows = slice(d * CAP + n, d * CAP + n + CHUNK)
        s = s_ref[n : n + CHUNK, j * IMG : (j + 1) * IMG]
        w = jnp.exp2(s - r) + jnp.exp2(s - wide(c_ref[rows, :], IMG))
        w = w - jnp.where(wide(column_ref[rows, :], IMG) == ids, weight, 0.0)
        high = w.astype(BF16)
        high_ref[n : n + CHUNK, :] = high
        low_ref[n : n + CHUNK, :] = (w - high.astype(F32)).astype(BF16)


TERMS = [pltpu.VMEM((CAP, IMG), BF16)] * 4


def text_kernel(
    d, base_ref, s_ref, x_ref, r_ref, c_ref, column_ref, weight_ref, o_ref, *terms
):
    acc = None
    for j in range(4):
        x = x_ref[j * IMG : (j + 1) * IMG, :]
        parts = terms[j % 2 * 2 : j % 2 * 2 + 2]
        split_weights(d, j, base_ref, s_ref, r_ref, c_ref, column_ref, weight_ref, *parts)
        for part in parts:
            term = jnp.dot(part[...], x, preferred_element_type=F32)
            acc = term if acc is None else acc + term
    o_ref[...] = acc


def text_terms(d, base, s, images, r, c, column, weight):
    return call(
        functools.partial(text_kernel, d),
        [((CAP, WIDTH), F32)],
        (base, s, images, r, c, column, weight),
        smem=1,
        scratch=TERMS,
    )[0]


def image_kernel(
    js, base_ref, s0, s1, s2, s3, t0, t1, t2, t3, r_ref, c_ref, column_ref, weight_ref, *refs
):
    outs, terms = refs[: len(js)], refs[len(js) :]
    for j, y in zip(js, outs):
        acc = None
        for d, (s_ref, t) in enumerate(((s0, t0), (s1, t1), (s2, t2), (s3, t3))):
            parts = terms[d % 2 * 2 : d % 2 * 2 + 2]
            split_weights(d, j, base_ref, s_ref, r_ref, c_ref, column_ref, weight_ref, *parts)
            for part in parts:
                term = lax.dot_general(
                    part[...], t[...], (((0,), (0,)), ((), ())), preferred_element_type=F32
                )
                acc = term if acc is None else acc + term
        y[...] = acc


def image_terms(js, base, s, texts, r, c, column, weight):
    return call(
        functools.partial(image_kernel, js),
        [((IMG, WIDTH), F32)] * len(js),
        (base, *s, *texts, r, c, column, weight),
        smem=1,
        scratch=TERMS,
    )


def after(*values):
    return lax.optimization_barrier(values)


def pack(value):
    return (value * SEND_SCALE).astype(jnp.float16)


def unpack(value):
    return value.astype(F32) * (1.0 / SEND_SCALE)


def shards(images, captions, cap_target, cap_count):
    groups = lax.axis_size("dp")
    blocks = lax.axis_size("blk")
    group_images = float(IMG * blocks)
    me = lax.axis_index("blk")
    my_x, my_yc = lax.div(me, 4), lax.rem(me, 4)

    image1 = across(images, 1)
    image2 = across(images, 2)
    received = lax.all_to_all(captions, "dp", split_axis=0, concat_axis=0, tiled=True)
    image3 = across(image2, 1)

    alive = (lax.iota(jnp.int32, SLOT)[None, :] < cap_count[0][:, None]).reshape(blocks, CAP)
    targets = jnp.where(alive, cap_target[0].reshape(blocks, CAP), -IMG * blocks).astype(F32)
    live = jnp.sum(cap_count[0]).astype(F32)
    half_balance = 0.5 * group_images / live
    order = jnp.stack([lax.rem(my_x + d, XS) * 4 + my_yc for d in range(4)])
    base = jnp.stack([(my_x * 4 + (my_yc ^ q)) * IMG for q in range(4)])
    scal = jnp.stack(
        [
            half_balance,
            jnp.float32(LN2 * 0.5 / group_images / groups),
            LN2 * 0.5 / live / groups,
            jnp.float32(LN2 / group_images / groups),
        ]
    )
    weight, column, mine = setup(base, order, half_balance[None], targets)
    received, weight, column, mine, scal = after(received, weight, column, mine, scal)
    texts = (received,) + tuple(along_x(received, -d) for d in (1, 2, 3))
    parts, column, weight = join((images, image1, image2, image3), column, weight)

    s, found = [None] * 4, []
    for d in (0, 1, 3, 2):
        s[d], img, cap = scores(d, base, parts, texts[d], column, weight, found if d == 2 else [])
        found += [img, cap]
    imgs = (img,) + tuple(across(img, q) for q in (1, 2, 3))
    caps = (cap,) + tuple(along_x(cap, e) for e in (1, 2, 3))
    r, c, loss_x, loss_yc = statistics(scal, imgs, caps, mine)
    loss_rows = loss_x.astype(jnp.float16)

    sent = [None] * 4
    for d in (2, 1, 3):
        part = pack(text_terms(d, base, s[d], parts, r, c, column, weight))
        part = jnp.concatenate([part, loss_rows], axis=0)
        sent[d] = along_x(part, d)
        r, part = after(r, part)
        if d == 2:
            r, loss_yc = after(r, loss_yc + across(loss_yc, 1))
        if d == 1:
            r, loss_yc = after(r, loss_yc)
            loss_yc = loss_yc + across(loss_yc, 2)
    y3, y1 = image_terms((3, 1), base, s, texts, r, c, column, weight)
    own = text_terms(0, base, s[0], parts, r, c, column, weight)
    r, own, loss_yc = after(r, own, loss_yc)
    y2, y0 = image_terms((2, 0), base, s, texts, r, c, column, weight)
    y3, y1, y2, y0, own, *sent = after(y3, y1, y2, y0, own, *sent[1:])
    a3, a1 = across(y3, 1), across(y1, 1)
    packed = pack(y2 + a3)
    text_grad = pack(own + sum(unpack(v[:CAP]) for v in sent))
    loss = loss_yc + loss_x[0:8, :128] + loss_x[8:16, :128]
    loss = loss + sum(v[CAP : CAP + 8, :128].astype(F32) + v[CAP + 8 :, :128].astype(F32) for v in sent)
    high = lax.reduce_precision(loss, 5, 10)
    lane = lax.broadcasted_iota(jnp.int32, loss.shape, 1)
    loss_lanes = jnp.where(lane < HALF, high, loss - high).astype(jnp.float16)
    loss_lanes = jnp.broadcast_to(loss_lanes[0:1], (CAP, 2 * HALF))
    text_grad = jnp.concatenate([text_grad, loss_lanes], axis=1)
    text_grad, packed = after(text_grad, packed)
    b = across(packed, 2)
    text_grad = lax.all_to_all(text_grad, "dp", split_axis=0, concat_axis=0, tiled=True)
    grad_captions = unpack(text_grad[:, :WIDTH]) * LOGIT_SCALE
    loss_value = jnp.sum(text_grad[:, WIDTH:].astype(F32)) / (SLOT * HALF)
    image_grad = (y0 + a1 + unpack(b)) * LOGIT_SCALE
    return loss_value, image_grad, grad_captions


def solution(mesh):
    return jax.shard_map(
        shards,
        mesh=mesh,
        in_specs=(P(("dp", "blk"), None), P(("dp", "blk"), None), P("dp", None), P("dp", None)),
        out_specs=(P(), P(("dp", "blk"), None), P(("dp", "blk"), None)),
        check_vma=False,
    )
```

```python
import functools
import math

import jax
import jax.numpy as jnp
from jax import lax
from jax.experimental import pallas as pl
from jax.experimental.pallas import tpu as pltpu
from jax.sharding import PartitionSpec as P

LOGIT_SCALE = 50.0
SCALE_LOG2 = LOGIT_SCALE * math.log2(math.e)
LN2 = math.log(2.0)
SEND_SCALE = 16.0
VERY_LOW = -1e30
VERY_HIGH = 3e38
VMEM_BYTES = 20 * 1024 * 1024
F32 = jnp.float32
BF16 = jnp.bfloat16

XS, YS, CORES = 4, 2, 2
IMG = 512
CAP = 256
WIDTH = 768
ROWS = 4 * IMG
SLOT = 16
HALF = 64
CHUNK = 32


def call(kernel, out, args, smem=0, scratch=()):
    vmem = pl.BlockSpec(memory_space=pltpu.VMEM)
    scalars = [pl.BlockSpec(memory_space=pltpu.SMEM)] * smem
    return pl.pallas_call(
        kernel,
        out_shape=tuple(jax.ShapeDtypeStruct(*o) for o in out),
        in_specs=scalars + [vmem] * (len(args) - smem),
        out_specs=(vmem,) * len(out),
        scratch_shapes=list(scratch),
        compiler_params=pltpu.CompilerParams(vmem_limit_bytes=VMEM_BYTES),
        cost_estimate=pl.CostEstimate(flops=1 << 20, bytes_accessed=1 << 16, transcendentals=0),
    )(*args)


def move(value, there):
    spots = [(x, y, c) for x in range(XS) for y in range(YS) for c in range(CORES)]
    flat = lambda x, y, c: (x * YS + y) * CORES + c
    return lax.ppermute(value, "blk", [(flat(*s), flat(*there(*s))) for s in spots])


def along_x(value, shift):
    return move(value, lambda x, y, c: ((x + shift) % XS, y, c))


def across(value, q):
    return move(value, lambda x, y, c: (x, y ^ (q >> 1), c ^ (q & 1)))


def row_of(column, lanes=128):
    return jnp.broadcast_to(column, (column.shape[0], lanes)).T[0:1, :]


def column_of(row, lanes=128):
    return jnp.broadcast_to(row, (lanes, row.shape[1])).T


def wide(column, lanes):
    return jnp.concatenate([column] * (lanes // column.shape[1]), axis=1)


def log_sum(parts):
    peak = functools.reduce(jnp.maximum, parts)
    return peak + jnp.log2(sum(jnp.exp2(p - peak) for p in parts))


def setup_kernel(
    base_ref, order_ref, counts_ref, targets_in, weight_ref, column_ref, mine_ref, scal_ref, targets_ref
):
    blocks = targets_ref.shape[0]
    iota = lambda shape, dim: lax.broadcasted_iota(jnp.int32, shape, dim)
    counts = counts_ref[...].astype(F32)
    live = jnp.sum(counts, axis=1, keepdims=True)
    half_balance = 0.5 * IMG * blocks / live
    scal_ref[0:1, :] = jnp.broadcast_to(half_balance, (1, 128))
    scal_ref[1:2, :] = jnp.broadcast_to(LN2 * 0.5 / blocks / live, (1, 128))
    scal_ref[2:8, :] = jnp.zeros((6, 128), F32)
    slot = iota((CAP, CAP), 1) // SLOT
    spread = jnp.where(iota((CAP, CAP), 0) % SLOT == slot, 1.0, 0.0).astype(BF16)
    owned = jnp.where(iota((blocks, CAP), 1) // SLOT == iota((blocks, CAP), 0), counts, 0.0)
    filled = jnp.dot(owned.astype(BF16), spread, preferred_element_type=F32)
    for b in range(blocks):
        targets_ref[b : b + 1, :] = targets_in[0:1, b * CAP : (b + 1) * CAP].astype(F32)
    alive = (iota((blocks, CAP), 1) % SLOT).astype(F32) < filled
    targets_ref[...] = jnp.where(alive, targets_ref[...], -1.0)
    mine_ref[...] = jnp.zeros_like(mine_ref)
    for d in range(4):
        row = targets_ref[pl.ds(order_ref[d], 1), :]
        mine_ref[d : d + 1, :] = row
        column_ref[d * CAP : (d + 1) * CAP, :] = column_of(row)
    weight_ref[...] = jnp.zeros_like(weight_ref)
    step = 256
    for i in range(ROWS // step):
        j, at = i * step // IMG, i * step % IMG
        ids = iota((step, 128), 0).astype(F32) + (base_ref[j] + at).astype(F32)

        def add(b, acc):
            row = targets_ref[pl.ds(b, 1), :]
            for h in range(CAP // 128):
                acc = acc + jnp.where(row[:, h * 128 : (h + 1) * 128] == ids, 1.0, 0.0)
            return acc

        hits = lax.fori_loop(0, blocks, add, jnp.zeros((step, 128), F32), unroll=2)
        count = jnp.sum(hits, axis=1, keepdims=True)
        weight_ref[j : j + 1, at : at + step] = row_of(0.5 / jnp.maximum(count, 1.0) + half_balance)


def setup(base, order, counts, targets):
    return call(
        setup_kernel,
        [((8, IMG), F32), ((4 * CAP, 128), F32), ((8, CAP), F32), ((8, 128), F32)],
        (base, order, counts, targets),
        smem=2,
        scratch=[pltpu.VMEM((targets.shape[1] // CAP, CAP), F32)],
    )


def join_kernel(x0, x1, x2, x3, *refs):
    ins, (x_ref, *outs) = refs[: len(refs) // 2], refs[len(refs) // 2 :]
    for j, x in enumerate((x0, x1, x2, x3)):
        x_ref[j * IMG : (j + 1) * IMG, :] = x[...]
    for i, o in zip(ins, outs):
        o[...] = i[...]


def join(images, *others):
    return call(
        join_kernel,
        [((ROWS, WIDTH), BF16)] + [(o.shape, o.dtype) for o in others],
        (*images, *others),
    )


def tiles(s):
    return [s[:, n : n + 128] for n in range(0, s.shape[1], 128)]


def fold(op, s):
    return functools.reduce(op, [s[n : n + 8, :] for n in range(0, s.shape[0], 8)])


def scores_kernel(d, n_others, base_ref, *refs):
    (x_ref, t_ref, column_ref, weight_ref), refs = refs[:4], refs[4:]
    others, refs = refs[: 2 * n_others], refs[2 * n_others :]
    s_ref, img_ref, cap_ref, dots0, dots1, peak, mass = refs
    img_ref[...] = jnp.zeros_like(img_ref)
    hits = jnp.zeros((8, IMG), F32)
    for j in range(4):
        cols = slice(j * IMG, (j + 1) * IMG)
        dots = (dots0, dots1)[j % 2]
        dots[...] = lax.dot_general(
            t_ref[...], x_ref[cols, :], (((1,), (1,)), ((), ())), preferred_element_type=F32
        )
        ids = (lax.broadcasted_iota(jnp.int32, (1, IMG), 1) + base_ref[j]).astype(F32)
        weight = weight_ref[j : j + 1, :]
        top = jnp.full((8, IMG), -VERY_HIGH, F32)
        for n in range(0, CAP, CHUNK):
            at = slice(n, n + CHUNK)
            target = column_ref[d * CAP + n : d * CAP + n + CHUNK, :]
            limit = wide(jnp.where(target < 0.0, VERY_LOW, VERY_HIGH), IMG)
            s = jnp.minimum(dots[at, :] * SCALE_LOG2, limit)
            s_ref[at, cols] = s
            top = jnp.maximum(top, fold(jnp.maximum, s))
            hits = hits + fold(jnp.add, jnp.where(wide(target, IMG) == ids, s * weight, 0.0))
            new = functools.reduce(jnp.maximum, tiles(s))
            if j:
                old = peak[at, :]
                new = jnp.maximum(new, old)
                mass[at, :] = mass[at, :] * jnp.exp2(old - new)
            peak[at, :] = new
        top = jnp.max(top, axis=0, keepdims=True)
        total = jnp.zeros((8, IMG), F32)
        for n in range(0, CAP, CHUNK):
            at = slice(n, n + CHUNK)
            s = s_ref[at, cols]
            total = total + fold(jnp.add, jnp.exp2(s - top))
            add = sum(jnp.exp2(p - peak[at, :]) for p in tiles(s))
            mass[at, :] = mass[at, :] + add if j else add
        img_ref[j : j + 1, :] = top + jnp.log2(jnp.sum(total, axis=0, keepdims=True))
    img_ref[4:5, :] = jnp.sum(hits, axis=0, keepdims=True)
    top = jnp.max(peak[...], axis=1, keepdims=True)
    total = jnp.sum(mass[...] * jnp.exp2(peak[...] - top), axis=1, keepdims=True)
    cap_ref[...] = jnp.zeros_like(cap_ref)
    cap_ref[d : d + 1, :] = row_of(top + jnp.log2(total))
    if others:
        img, cap = others[0::2], others[1::2]
        img_ref[0:4, :] = log_sum([img_ref[0:4, :]] + [o[0:4, :] for o in img])
        img_ref[4:5, :] = sum((o[4:5, :] for o in img), img_ref[4:5, :])
        cap_ref[...] = sum((o[...] for o in cap), cap_ref[...])


def scores(d, base, images, text, column, weight, others):
    return call(
        functools.partial(scores_kernel, d, len(others) // 2),
        [((CAP, ROWS), F32), ((8, IMG), F32), ((8, CAP), F32)],
        (base, images, text, column, weight, *others),
        smem=1,
        scratch=[pltpu.VMEM((CAP, IMG), F32)] * 2 + [pltpu.VMEM((CAP, 128), F32)] * 2,
    )


def stats_kernel(
    share, scal_ref, img0, img1, img2, img3, cap0, cap1, cap2, cap3, mine_ref, r_ref, c_ref, a_ref, b_ref
):
    pick = lambda ref, order: jnp.concatenate([ref[o : o + 1, :] for o in order], axis=0)
    imgs, caps = (img0, img1, img2, img3), (cap0, cap1, cap2, cap3)
    r = log_sum([pick(ref, [j ^ q for j in range(4)]) for q, ref in enumerate(imgs)])
    r_ref[0:4, :] = r + 1.0
    r_ref[4:8, :] = jnp.zeros((4, IMG), F32)
    alive = mine_ref[0:4, :] >= 0.0
    c = log_sum([pick(ref, [(d + e) % 4 for d in range(4)]) for e, ref in enumerate(caps)])
    c = jnp.where(alive, c, 0.0)
    moved = jnp.where(alive, c - jnp.log2(scal_ref[0:1, 0:1]), 0.0)
    for d in range(4):
        c_ref[d * CAP : (d + 1) * CAP, :] = column_of(moved[d : d + 1, :])
    hits = sum(ref[4:5, :] for ref in imgs)
    a = (jnp.sum(r) * 0.5 - jnp.sum(hits)) * (LN2 / share)
    a = jnp.full((8, WIDTH), a, F32)
    high = a.astype(BF16).astype(F32)
    a_ref[0:8, :] = high
    a_ref[8:16, :] = a - high
    b_ref[...] = jnp.broadcast_to(jnp.sum(c) * scal_ref[1:2, :], (8, 128))


def statistics(share, scal, imgs, caps, mine):
    return call(
        functools.partial(stats_kernel, share),
        [((8, IMG), F32), ((4 * CAP, 128), F32), ((16, WIDTH), F32), ((8, 128), F32)],
        (scal, *imgs, *caps, mine),
    )


def split_weights(d, j, base_ref, s_ref, r_ref, c_ref, column_ref, weight_ref, high_ref, low_ref):
    ids = (lax.broadcasted_iota(jnp.int32, (1, IMG), 1) + base_ref[j]).astype(F32)
    r = r_ref[j : j + 1, :]
    weight = weight_ref[j : j + 1, :]
    for n in range(0, CAP, CHUNK):
        rows = slice(d * CAP + n, d * CAP + n + CHUNK)
        s = s_ref[n : n + CHUNK, j * IMG : (j + 1) * IMG]
        w = jnp.exp2(s - r) + jnp.exp2(s - wide(c_ref[rows, :], IMG))
        w = w - jnp.where(wide(column_ref[rows, :], IMG) == ids, weight, 0.0)
        high = w.astype(BF16)
        high_ref[n : n + CHUNK, :] = high
        low_ref[n : n + CHUNK, :] = (w - high.astype(F32)).astype(BF16)


TERMS = [pltpu.VMEM((CAP, IMG), BF16)] * 4


def text_kernel(
    d, base_ref, s_ref, x_ref, r_ref, c_ref, column_ref, weight_ref, o_ref, *terms
):
    acc = None
    for j in range(4):
        x = x_ref[j * IMG : (j + 1) * IMG, :]
        parts = terms[j % 2 * 2 : j % 2 * 2 + 2]
        split_weights(d, j, base_ref, s_ref, r_ref, c_ref, column_ref, weight_ref, *parts)
        for part in parts:
            term = jnp.dot(part[...], x, preferred_element_type=F32)
            acc = term if acc is None else acc + term
    o_ref[...] = acc


def text_terms(d, base, s, images, r, c, column, weight):
    return call(
        functools.partial(text_kernel, d),
        [((CAP, WIDTH), F32)],
        (base, s, images, r, c, column, weight),
        smem=1,
        scratch=TERMS,
    )[0]


def image_kernel(
    js, base_ref, s0, s1, s2, s3, t0, t1, t2, t3, r_ref, c_ref, column_ref, weight_ref, *refs
):
    outs, terms = refs[: len(js)], refs[len(js) :]
    for j, y in zip(js, outs):
        acc = None
        for d, (s_ref, t) in enumerate(((s0, t0), (s1, t1), (s2, t2), (s3, t3))):
            parts = terms[d % 2 * 2 : d % 2 * 2 + 2]
            split_weights(d, j, base_ref, s_ref, r_ref, c_ref, column_ref, weight_ref, *parts)
            for part in parts:
                term = lax.dot_general(
                    part[...], t[...], (((0,), (0,)), ((), ())), preferred_element_type=F32
                )
                acc = term if acc is None else acc + term
        y[...] = acc


def image_terms(js, base, s, texts, r, c, column, weight):
    return call(
        functools.partial(image_kernel, js),
        [((IMG, WIDTH), F32)] * len(js),
        (base, *s, *texts, r, c, column, weight),
        smem=1,
        scratch=TERMS,
    )


def after(*values):
    return lax.optimization_barrier(values)


def pack(value):
    return (value * SEND_SCALE).astype(jnp.float16)


def unpack(value):
    return value.astype(F32) * (1.0 / SEND_SCALE)


def shards(images, captions, cap_target, cap_count):
    groups = lax.axis_size("dp")
    blocks = lax.axis_size("blk")
    me = lax.axis_index("blk")
    my_x, my_yc = lax.div(me, 4), lax.rem(me, 4)
    order = jnp.stack([lax.rem(my_x + d, XS) * 4 + my_yc for d in range(4)])
    base = jnp.stack([(my_x * 4 + (my_yc ^ q)) * IMG for q in range(4)])

    image1 = across(images, 1)
    image2 = across(images, 2)
    received = lax.all_to_all(captions, "dp", split_axis=0, concat_axis=0, tiled=True)
    weight, column, mine, scal = setup(base, order, cap_count, cap_target)
    image2, weight, column, mine, scal = after(image2, weight, column, mine, scal)
    image3 = across(image2, 1)
    texts = (received,) + tuple(along_x(received, -d) for d in (1, 2, 3))
    images = (images, image1, image2, image3)
    parts, column, weight, mine, scal = join(images, column, weight, mine, scal)

    s, found = [None] * 4, []
    for d in (0, 1, 3, 2):
        s[d], img, cap = scores(d, base, parts, texts[d], column, weight, found if d == 2 else [])
        found += [img, cap]
    imgs = (img,) + tuple(across(img, q) for q in (1, 2, 3))
    caps = (cap,) + tuple(along_x(cap, e) for e in (1, 2, 3))
    r, c, loss_x, loss_yc = statistics(IMG * blocks * groups, scal, imgs, caps, mine)
    loss_rows = loss_x.astype(jnp.float16)

    loss_yc = loss_yc + across(loss_yc, 2)
    (y3,) = image_terms((3,), base, s, texts, r, c, column, weight)
    a3 = across(pack(y3), 1)
    r, y3 = after(r, y3)
    (y2,) = image_terms((2,), base, s, texts, r, c, column, weight)
    packed = pack(y2 + unpack(a3))
    b = across(packed, 2)
    r, packed, loss_yc = after(r, packed, loss_yc)
    sent = [None] * 4
    for d in (2, 1, 3):
        part = pack(text_terms(d, base, s[d], parts, r, c, column, weight))
        part = jnp.concatenate([part, loss_rows], axis=0)
        sent[d] = along_x(part, d)
        r, part = after(r, part)
    own = text_terms(0, base, s[0], parts, r, c, column, weight)
    r, own = after(r, own)
    y1, y0 = image_terms((1, 0), base, s, texts, r, c, column, weight)
    a1 = across(pack(y1), 1)
    sent = sent[1:]
    loss_yc, sent[1], b = after(loss_yc, sent[1], b)
    loss_yc = loss_yc + across(loss_yc, 1)
    text_grad = pack(own + sum(unpack(v[:CAP]) for v in sent))
    loss = loss_yc + loss_x[0:8, :128] + loss_x[8:16, :128]
    loss = loss + sum(v[CAP : CAP + 8, :128].astype(F32) + v[CAP + 8 :, :128].astype(F32) for v in sent)
    high = lax.reduce_precision(loss, 5, 10)
    lane = lax.broadcasted_iota(jnp.int32, loss.shape, 1)
    loss_lanes = jnp.where(lane < HALF, high, loss - high).astype(jnp.float16)
    loss_lanes = jnp.broadcast_to(loss_lanes[0:1], (CAP, 2 * HALF))
    text_grad = jnp.concatenate([text_grad, loss_lanes], axis=1)
    text_grad, y0, b = after(text_grad, y0, b)
    text_grad = lax.all_to_all(text_grad, "dp", split_axis=0, concat_axis=0, tiled=True)
    grad_captions = unpack(text_grad[:, :WIDTH]) * LOGIT_SCALE
    loss_value = jnp.sum(text_grad[:, WIDTH:].astype(F32)) / (SLOT * HALF)
    image_grad = (y0 + unpack(a1) + unpack(b)) * LOGIT_SCALE
    return loss_value, image_grad, grad_captions


def solution(mesh):
    return jax.shard_map(
        shards,
        mesh=mesh,
        in_specs=(P(("dp", "blk"), None), P(("dp", "blk"), None), P("dp", None), P("dp", None)),
        out_specs=(P(), P(("dp", "blk"), None), P(("dp", "blk"), None)),
        check_vma=False,
    )
```

```python
import functools
import math

import jax
import jax.numpy as jnp
from jax import lax
from jax.experimental import pallas as pl
from jax.experimental.pallas import tpu as pltpu
from jax.sharding import PartitionSpec as P

LOGIT_SCALE = 50.0
SCALE_LOG2 = LOGIT_SCALE * math.log2(math.e)
LN2 = math.log(2.0)
SEND_SCALE = 16.0
VERY_LOW = -1e30
VERY_HIGH = 3e38
VMEM_BYTES = 20 * 1024 * 1024
F32 = jnp.float32
BF16 = jnp.bfloat16

XS, YS, CORES = 4, 2, 2
IMG = 512
CAP = 256
WIDTH = 768
ROWS = 4 * IMG
SLOT = 16
HALF = 64
CHUNK = 32


def call(kernel, out, args, smem=0, scratch=()):
    vmem = pl.BlockSpec(memory_space=pltpu.VMEM)
    scalars = [pl.BlockSpec(memory_space=pltpu.SMEM)] * smem
    return pl.pallas_call(
        kernel,
        out_shape=tuple(jax.ShapeDtypeStruct(*o) for o in out),
        in_specs=scalars + [vmem] * (len(args) - smem),
        out_specs=(vmem,) * len(out),
        scratch_shapes=list(scratch),
        compiler_params=pltpu.CompilerParams(vmem_limit_bytes=VMEM_BYTES),
        cost_estimate=pl.CostEstimate(flops=1 << 20, bytes_accessed=1 << 16, transcendentals=0),
    )(*args)


def move(value, there):
    spots = [(x, y, c) for x in range(XS) for y in range(YS) for c in range(CORES)]
    flat = lambda x, y, c: (x * YS + y) * CORES + c
    return lax.ppermute(value, "blk", [(flat(*s), flat(*there(*s))) for s in spots])


def along_x(value, shift):
    return move(value, lambda x, y, c: ((x + shift) % XS, y, c))


def across(value, q):
    return move(value, lambda x, y, c: (x, y ^ (q >> 1), c ^ (q & 1)))


def row_of(column, lanes=128):
    return jnp.broadcast_to(column, (column.shape[0], lanes)).T[0:1, :]


def column_of(row, lanes=128):
    return jnp.broadcast_to(row, (lanes, row.shape[1])).T


def wide(column, lanes):
    return jnp.concatenate([column] * (lanes // column.shape[1]), axis=1)


def log_sum(parts):
    peak = functools.reduce(jnp.maximum, parts)
    return peak + jnp.log2(sum(jnp.exp2(p - peak) for p in parts))


def setup_kernel(
    base_ref, order_ref, counts_ref, targets_in, weight_ref, column_ref, limit_ref, mine_ref, scal_ref, targets_ref
):
    blocks = targets_ref.shape[0]
    iota = lambda shape, dim: lax.broadcasted_iota(jnp.int32, shape, dim)
    counts = counts_ref[...].astype(F32)
    live = jnp.sum(counts, axis=1, keepdims=True)
    half_balance = 0.5 * IMG * blocks / live
    scal_ref[0:1, :] = jnp.broadcast_to(half_balance, (1, 128))
    scal_ref[1:2, :] = jnp.broadcast_to(LN2 * 0.5 / blocks / live, (1, 128))
    scal_ref[2:8, :] = jnp.zeros((6, 128), F32)
    slot = iota((CAP, CAP), 1) // SLOT
    spread = jnp.where(iota((CAP, CAP), 0) % SLOT == slot, 1.0, 0.0).astype(BF16)
    owned = jnp.where(iota((blocks, CAP), 1) // SLOT == iota((blocks, CAP), 0), counts, 0.0)
    filled = jnp.dot(owned.astype(BF16), spread, preferred_element_type=F32)
    for b in range(blocks):
        targets_ref[b : b + 1, :] = targets_in[0:1, b * CAP : (b + 1) * CAP].astype(F32)
    alive = (iota((blocks, CAP), 1) % SLOT).astype(F32) < filled
    targets_ref[...] = jnp.where(alive, targets_ref[...], -1.0)
    mine_ref[...] = jnp.zeros_like(mine_ref)
    for d in range(4):
        row = targets_ref[pl.ds(order_ref[d], 1), :]
        mine_ref[d : d + 1, :] = row
        place = jnp.full_like(row, -1.0)
        for j in range(4):
            at = row - base_ref[j].astype(F32)
            place = jnp.where((at >= 0.0) & (at < IMG), at + j * IMG, place)
        column_ref[d * CAP : (d + 1) * CAP, :] = column_of(place)
        limit_ref[d * CAP : (d + 1) * CAP, :] = column_of(jnp.where(row < 0.0, VERY_LOW, VERY_HIGH))
    weight_ref[...] = jnp.zeros_like(weight_ref)
    step = 256
    for i in range(ROWS // step):
        j, at = i * step // IMG, i * step % IMG
        ids = iota((step, 128), 0).astype(F32) + (base_ref[j] + at).astype(F32)

        def add(b, acc):
            row = targets_ref[pl.ds(b, 1), :]
            for h in range(CAP // 128):
                acc = acc + jnp.where(row[:, h * 128 : (h + 1) * 128] == ids, 1.0, 0.0)
            return acc

        hits = lax.fori_loop(0, blocks, add, jnp.zeros((step, 128), F32), unroll=2)
        count = jnp.sum(hits, axis=1, keepdims=True)
        weight_ref[j : j + 1, at : at + step] = row_of(0.5 / jnp.maximum(count, 1.0) + half_balance)


def setup(base, order, counts, targets):
    return call(
        setup_kernel,
        [((8, IMG), F32)] + [((4 * CAP, 128), F32)] * 2 + [((8, CAP), F32), ((8, 128), F32)],
        (base, order, counts, targets),
        smem=2,
        scratch=[pltpu.VMEM((targets.shape[1] // CAP, CAP), F32)],
    )


def join_kernel(x0, x1, x2, x3, *refs):
    ins, (x_ref, *outs) = refs[: len(refs) // 2], refs[len(refs) // 2 :]
    for j, x in enumerate((x0, x1, x2, x3)):
        x_ref[j * IMG : (j + 1) * IMG, :] = x[...]
    for i, o in zip(ins, outs):
        o[...] = i[...]


def join(images, *others):
    return call(
        join_kernel,
        [((ROWS, WIDTH), BF16)] + [(o.shape, o.dtype) for o in others],
        (*images, *others),
    )


def tiles(s):
    return [s[:, n : n + 128] for n in range(0, s.shape[1], 128)]


def fold(op, s):
    return functools.reduce(op, [s[n : n + 8, :] for n in range(0, s.shape[0], 8)])


def scores_kernel(d, n_others, *refs):
    (x_ref, t_ref, column_ref, limit_ref, weight_ref), refs = refs[:5], refs[5:]
    others, refs = refs[: 2 * n_others], refs[2 * n_others :]
    s_ref, img_ref, cap_ref, dots0, dots1, peak, mass = refs
    img_ref[...] = jnp.zeros_like(img_ref)
    hits = jnp.zeros((8, IMG), F32)
    for j in range(4):
        cols = slice(j * IMG, (j + 1) * IMG)
        dots = (dots0, dots1)[j % 2]
        dots[...] = lax.dot_general(
            t_ref[...], x_ref[cols, :], (((1,), (1,)), ((), ())), preferred_element_type=F32
        )
        ids = (lax.broadcasted_iota(jnp.int32, (1, IMG), 1) + j * IMG).astype(F32)
        weight = weight_ref[j : j + 1, :]
        top = jnp.full((8, IMG), -VERY_HIGH, F32)
        for n in range(0, CAP, CHUNK):
            at = slice(n, n + CHUNK)
            target = column_ref[d * CAP + n : d * CAP + n + CHUNK, :]
            limit = wide(limit_ref[d * CAP + n : d * CAP + n + CHUNK, :], IMG)
            s = jnp.minimum(dots[at, :] * SCALE_LOG2, limit)
            s_ref[at, cols] = s
            top = jnp.maximum(top, fold(jnp.maximum, s))
            hits = hits + fold(jnp.add, jnp.where(wide(target, IMG) == ids, s * weight, 0.0))
            new = functools.reduce(jnp.maximum, tiles(s))
            if j:
                old = peak[at, :]
                new = jnp.maximum(new, old)
                mass[at, :] = mass[at, :] * jnp.exp2(old - new)
            peak[at, :] = new
        top = jnp.max(top, axis=0, keepdims=True)
        total = jnp.zeros((8, IMG), F32)
        for n in range(0, CAP, CHUNK):
            at = slice(n, n + CHUNK)
            s = s_ref[at, cols]
            total = total + fold(jnp.add, jnp.exp2(s - top))
            add = sum(jnp.exp2(p - peak[at, :]) for p in tiles(s))
            mass[at, :] = mass[at, :] + add if j else add
        img_ref[j : j + 1, :] = top + jnp.log2(jnp.sum(total, axis=0, keepdims=True))
    img_ref[4:5, :] = jnp.sum(hits, axis=0, keepdims=True)
    top = jnp.max(peak[...], axis=1, keepdims=True)
    total = jnp.sum(mass[...] * jnp.exp2(peak[...] - top), axis=1, keepdims=True)
    cap_ref[...] = jnp.zeros_like(cap_ref)
    cap_ref[d : d + 1, :] = row_of(top + jnp.log2(total))
    if others:
        img, cap = others[0::2], others[1::2]
        img_ref[0:4, :] = log_sum([img_ref[0:4, :]] + [o[0:4, :] for o in img])
        img_ref[4:5, :] = sum((o[4:5, :] for o in img), img_ref[4:5, :])
        cap_ref[...] = sum((o[...] for o in cap), cap_ref[...])


def scores(d, images, text, column, limit, weight, others):
    return call(
        functools.partial(scores_kernel, d, len(others) // 2),
        [((CAP, ROWS), F32), ((8, IMG), F32), ((8, CAP), F32)],
        (images, text, column, limit, weight, *others),
        scratch=[pltpu.VMEM((CAP, IMG), F32)] * 2 + [pltpu.VMEM((CAP, 128), F32)] * 2,
    )


def stats_kernel(
    share, scal_ref, img0, img1, img2, img3, cap0, cap1, cap2, cap3, mine_ref, r_ref, c_ref, a_ref, b_ref
):
    pick = lambda ref, order: jnp.concatenate([ref[o : o + 1, :] for o in order], axis=0)
    imgs, caps = (img0, img1, img2, img3), (cap0, cap1, cap2, cap3)
    r = log_sum([pick(ref, [j ^ q for j in range(4)]) for q, ref in enumerate(imgs)])
    r_ref[0:4, :] = r + 1.0
    r_ref[4:8, :] = jnp.zeros((4, IMG), F32)
    alive = mine_ref[0:4, :] >= 0.0
    c = log_sum([pick(ref, [(d + e) % 4 for d in range(4)]) for e, ref in enumerate(caps)])
    c = jnp.where(alive, c, 0.0)
    moved = jnp.where(alive, c - jnp.log2(scal_ref[0:1, 0:1]), 0.0)
    for d in range(4):
        c_ref[d * CAP : (d + 1) * CAP, :] = column_of(moved[d : d + 1, :])
    hits = sum(ref[4:5, :] for ref in imgs)
    a = (jnp.sum(r) * 0.5 - jnp.sum(hits)) * (LN2 / share)
    a = jnp.full((8, WIDTH), a, F32)
    high = a.astype(BF16).astype(F32)
    a_ref[0:8, :] = high
    a_ref[8:16, :] = a - high
    b_ref[...] = jnp.broadcast_to(jnp.sum(c) * scal_ref[1:2, :], (8, 128))


def statistics(share, scal, imgs, caps, mine):
    return call(
        functools.partial(stats_kernel, share),
        [((8, IMG), F32), ((4 * CAP, 128), F32), ((16, WIDTH), F32), ((8, 128), F32)],
        (scal, *imgs, *caps, mine),
    )


def split_weights(d, j, s_ref, r_ref, c_ref, column_ref, weight_ref, high_ref, low_ref):
    ids = (lax.broadcasted_iota(jnp.int32, (1, IMG), 1) + j * IMG).astype(F32)
    r = r_ref[j : j + 1, :]
    weight = weight_ref[j : j + 1, :]
    for n in range(0, CAP, CHUNK):
        rows = slice(d * CAP + n, d * CAP + n + CHUNK)
        s = s_ref[n : n + CHUNK, j * IMG : (j + 1) * IMG]
        w = jnp.exp2(s - r) + jnp.exp2(s - wide(c_ref[rows, :], IMG))
        w = w - jnp.where(wide(column_ref[rows, :], IMG) == ids, weight, 0.0)
        high = w.astype(BF16)
        high_ref[n : n + CHUNK, :] = high
        low_ref[n : n + CHUNK, :] = (w - high.astype(F32)).astype(BF16)


TERMS = [pltpu.VMEM((CAP, IMG), BF16)] * 4


def text_kernel(
    d, s_ref, x_ref, r_ref, c_ref, column_ref, weight_ref, o_ref, *terms
):
    acc = None
    for j in range(4):
        x = x_ref[j * IMG : (j + 1) * IMG, :]
        parts = terms[j % 2 * 2 : j % 2 * 2 + 2]
        split_weights(d, j, s_ref, r_ref, c_ref, column_ref, weight_ref, *parts)
        for part in parts:
            term = jnp.dot(part[...], x, preferred_element_type=F32)
            acc = term if acc is None else acc + term
    o_ref[...] = acc


def text_terms(d, s, images, r, c, column, weight):
    return call(
        functools.partial(text_kernel, d),
        [((CAP, WIDTH), F32)],
        (s, images, r, c, column, weight),
        scratch=TERMS,
    )[0]


def image_kernel(
    js, s0, s1, s2, s3, t0, t1, t2, t3, r_ref, c_ref, column_ref, weight_ref, *refs
):
    outs, terms = refs[: len(js)], refs[len(js) :]
    for j, y in zip(js, outs):
        acc = None
        for d, (s_ref, t) in enumerate(((s0, t0), (s1, t1), (s2, t2), (s3, t3))):
            parts = terms[d % 2 * 2 : d % 2 * 2 + 2]
            split_weights(d, j, s_ref, r_ref, c_ref, column_ref, weight_ref, *parts)
            for part in parts:
                term = lax.dot_general(
                    part[...], t[...], (((0,), (0,)), ((), ())), preferred_element_type=F32
                )
                acc = term if acc is None else acc + term
        y[...] = acc


def image_terms(js, s, texts, r, c, column, weight):
    return call(
        functools.partial(image_kernel, js),
        [((IMG, WIDTH), F32)] * len(js),
        (*s, *texts, r, c, column, weight),
        scratch=TERMS,
    )


def after(*values):
    return lax.optimization_barrier(values)


def pack(value):
    return (value * SEND_SCALE).astype(jnp.float16)


def unpack(value):
    return value.astype(F32) * (1.0 / SEND_SCALE)


def shards(images, captions, cap_target, cap_count):
    groups = lax.axis_size("dp")
    blocks = lax.axis_size("blk")
    me = lax.axis_index("blk")
    my_x, my_yc = lax.div(me, 4), lax.rem(me, 4)
    order = jnp.stack([lax.rem(my_x + d, XS) * 4 + my_yc for d in range(4)])
    base = jnp.stack([(my_x * 4 + (my_yc ^ q)) * IMG for q in range(4)])

    image1 = across(images, 1)
    image2 = across(images, 2)
    received = lax.all_to_all(captions, "dp", split_axis=0, concat_axis=0, tiled=True)
    weight, column, limit, mine, scal = setup(base, order, cap_count, cap_target)
    image2, weight, column, limit, mine, scal = after(image2, weight, column, limit, mine, scal)
    image3 = across(image2, 1)
    images = (images, image1, image2, image3)
    parts, column, limit, weight, mine, scal = join(images, column, limit, weight, mine, scal)
    texts = (received,) + tuple(along_x(received, -d) for d in (1, 2, 3))

    s, found = [None] * 4, []
    for d in (0, 1, 3, 2):
        s[d], img, cap = scores(d, parts, texts[d], column, limit, weight, found if d == 2 else [])
        found += [img, cap]
    imgs = (img,) + tuple(across(img, q) for q in (1, 2, 3))
    caps = (cap,) + tuple(along_x(cap, e) for e in (1, 2, 3))
    r, c, loss_x, loss_yc = statistics(IMG * blocks * groups, scal, imgs, caps, mine)
    loss_rows = loss_x.astype(jnp.float16)

    loss_yc = loss_yc + across(loss_yc, 2)
    (y3,) = image_terms((3,), s, texts, r, c, column, weight)
    a3 = across(pack(y3), 1)
    r, y3 = after(r, y3)
    (y2,) = image_terms((2,), s, texts, r, c, column, weight)
    packed = pack(y2 + unpack(a3))
    b = across(packed, 2)
    r, packed, loss_yc = after(r, packed, loss_yc)
    sent = [None] * 4
    for d in (2, 1, 3):
        part = pack(text_terms(d, s[d], parts, r, c, column, weight))
        part = jnp.concatenate([part, loss_rows], axis=0)
        sent[d] = along_x(part, d)
        r, part = after(r, part)
    own = text_terms(0, s[0], parts, r, c, column, weight)
    r, own = after(r, own)
    y1, y0 = image_terms((1, 0), s, texts, r, c, column, weight)
    a1 = across(pack(y1), 1)
    sent = sent[1:]
    loss_yc, sent[1], b = after(loss_yc, sent[1], b)
    loss_yc = loss_yc + across(loss_yc, 1)
    text_grad = pack(own + sum(unpack(v[:CAP]) for v in sent))
    loss = loss_yc + loss_x[0:8, :128] + loss_x[8:16, :128]
    loss = loss + sum(v[CAP : CAP + 8, :128].astype(F32) + v[CAP + 8 :, :128].astype(F32) for v in sent)
    high = lax.reduce_precision(loss, 5, 10)
    lane = lax.broadcasted_iota(jnp.int32, loss.shape, 1)
    loss_lanes = jnp.where(lane < HALF, high, loss - high).astype(jnp.float16)
    loss_lanes = jnp.broadcast_to(loss_lanes[0:1], (CAP, 2 * HALF))
    text_grad = jnp.concatenate([text_grad, loss_lanes], axis=1)
    text_grad, y0, b = after(text_grad, y0, b)
    text_grad = lax.all_to_all(text_grad, "dp", split_axis=0, concat_axis=0, tiled=True)
    grad_captions = unpack(text_grad[:, :WIDTH]) * LOGIT_SCALE
    loss_value = jnp.sum(text_grad[:, WIDTH:].astype(F32)) / (SLOT * HALF)
    image_grad = (y0 + unpack(a1) + unpack(b)) * LOGIT_SCALE
    return loss_value, image_grad, grad_captions


def solution(mesh):
    return jax.shard_map(
        shards,
        mesh=mesh,
        in_specs=(P(("dp", "blk"), None), P(("dp", "blk"), None), P("dp", None), P("dp", None)),
        out_specs=(P(), P(("dp", "blk"), None), P(("dp", "blk"), None)),
        check_vma=False,
    )
```

```python
import functools
import math

import jax
import jax.numpy as jnp
from jax import lax
from jax.experimental import pallas as pl
from jax.experimental.pallas import tpu as pltpu
from jax.sharding import PartitionSpec as P

LOGIT_SCALE = 50.0
SCALE_LOG2 = LOGIT_SCALE * math.log2(math.e)
LN2 = math.log(2.0)
SEND_SCALE = 16.0
VERY_LOW = -1e30
VERY_HIGH = 3e38
VMEM_BYTES = 20 * 1024 * 1024
F32 = jnp.float32
BF16 = jnp.bfloat16

XS, YS, CORES = 4, 2, 2
IMG = 512
CAP = 256
WIDTH = 768
ROWS = 4 * IMG
SLOT = 16
HALF = 64
CHUNK = 32


def call(kernel, out, args, smem=0, scratch=()):
    vmem = pl.BlockSpec(memory_space=pltpu.VMEM)
    scalars = [pl.BlockSpec(memory_space=pltpu.SMEM)] * smem
    return pl.pallas_call(
        kernel,
        out_shape=tuple(jax.ShapeDtypeStruct(*o) for o in out),
        in_specs=scalars + [vmem] * (len(args) - smem),
        out_specs=(vmem,) * len(out),
        scratch_shapes=list(scratch),
        compiler_params=pltpu.CompilerParams(vmem_limit_bytes=VMEM_BYTES),
        cost_estimate=pl.CostEstimate(flops=1 << 20, bytes_accessed=1 << 16, transcendentals=0),
    )(*args)


def move(value, there):
    spots = [(x, y, c) for x in range(XS) for y in range(YS) for c in range(CORES)]
    flat = lambda x, y, c: (x * YS + y) * CORES + c
    return lax.ppermute(value, "blk", [(flat(*s), flat(*there(*s))) for s in spots])


def along_x(value, shift):
    return move(value, lambda x, y, c: ((x + shift) % XS, y, c))


def across(value, q):
    return move(value, lambda x, y, c: (x, y ^ (q >> 1), c ^ (q & 1)))


def row_of(column, lanes=128):
    return jnp.broadcast_to(column, (column.shape[0], lanes)).T[0:1, :]


def column_of(row, lanes=128):
    return jnp.broadcast_to(row, (lanes, row.shape[1])).T


def wide(column, lanes):
    return jnp.concatenate([column] * (lanes // column.shape[1]), axis=1)


def log_sum(parts):
    peak = functools.reduce(jnp.maximum, parts)
    return peak + jnp.log2(sum(jnp.exp2(p - peak) for p in parts))


def setup_kernel(
    base_ref, order_ref, counts_ref, targets_in, weight_ref, column_ref, limit_ref, mine_ref, scal_ref, targets_ref
):
    blocks = targets_ref.shape[0]
    iota = lambda shape, dim: lax.broadcasted_iota(jnp.int32, shape, dim)
    counts = counts_ref[...].astype(F32)
    live = jnp.sum(counts, axis=1, keepdims=True)
    half_balance = 0.5 * IMG * blocks / live
    scal_ref[0:1, :] = jnp.broadcast_to(half_balance, (1, 128))
    scal_ref[1:2, :] = jnp.broadcast_to(LN2 * 0.5 / blocks / live, (1, 128))
    scal_ref[2:8, :] = jnp.zeros((6, 128), F32)
    slot = iota((CAP, CAP), 1) // SLOT
    spread = jnp.where(iota((CAP, CAP), 0) % SLOT == slot, 1.0, 0.0).astype(BF16)
    owned = jnp.where(iota((blocks, CAP), 1) // SLOT == iota((blocks, CAP), 0), counts, 0.0)
    filled = jnp.dot(owned.astype(BF16), spread, preferred_element_type=F32)
    for b in range(blocks):
        targets_ref[b : b + 1, :] = targets_in[0:1, b * CAP : (b + 1) * CAP].astype(F32)
    alive = (iota((blocks, CAP), 1) % SLOT).astype(F32) < filled
    targets_ref[...] = jnp.where(alive, targets_ref[...], -1.0)
    mine_ref[...] = jnp.zeros_like(mine_ref)
    for d in range(4):
        row = targets_ref[pl.ds(order_ref[d], 1), :]
        mine_ref[d : d + 1, :] = row
        place = jnp.full_like(row, -1.0)
        for j in range(4):
            at = row - base_ref[j].astype(F32)
            place = jnp.where((at >= 0.0) & (at < IMG), at + j * IMG, place)
        column_ref[d * CAP : (d + 1) * CAP, :] = column_of(place)
        limit_ref[d * CAP : (d + 1) * CAP, :] = column_of(jnp.where(row < 0.0, VERY_LOW, VERY_HIGH))
    weight_ref[...] = jnp.zeros_like(weight_ref)
    step = 256
    for i in range(ROWS // step):
        j, at = i * step // IMG, i * step % IMG
        ids = iota((step, 128), 0).astype(F32) + (base_ref[j] + at).astype(F32)

        def add(b, acc):
            row = targets_ref[pl.ds(b, 1), :]
            for h in range(CAP // 128):
                acc = acc + jnp.where(row[:, h * 128 : (h + 1) * 128] == ids, 1.0, 0.0)
            return acc

        hits = lax.fori_loop(0, blocks, add, jnp.zeros((step, 128), F32), unroll=2)
        count = jnp.sum(hits, axis=1, keepdims=True)
        weight_ref[j : j + 1, at : at + step] = row_of(0.5 / jnp.maximum(count, 1.0) + half_balance)


def setup(base, order, counts, targets):
    return call(
        setup_kernel,
        [((8, IMG), F32)] + [((4 * CAP, 128), F32)] * 2 + [((8, CAP), F32), ((8, 128), F32)],
        (base, order, counts, targets),
        smem=2,
        scratch=[pltpu.VMEM((targets.shape[1] // CAP, CAP), F32)],
    )


def join_kernel(x0, x1, x2, x3, *refs):
    ins, (x_ref, *outs) = refs[: len(refs) // 2], refs[len(refs) // 2 :]
    for j, x in enumerate((x0, x1, x2, x3)):
        x_ref[j * IMG : (j + 1) * IMG, :] = x[...]
    for i, o in zip(ins, outs):
        o[...] = i[...]


def join(images, *others):
    return call(
        join_kernel,
        [((ROWS, WIDTH), BF16)] + [(o.shape, o.dtype) for o in others],
        (*images, *others),
    )


def tiles(s):
    return [s[:, n : n + 128] for n in range(0, s.shape[1], 128)]


def fold(op, s):
    return functools.reduce(op, [s[n : n + 8, :] for n in range(0, s.shape[0], 8)])


def scores_kernel(d, n_others, *refs):
    (x_ref, t_ref, column_ref, limit_ref, weight_ref), refs = refs[:5], refs[5:]
    others, refs = refs[: 2 * n_others], refs[2 * n_others :]
    s_ref, img_ref, cap_ref, dots0, dots1, peak, mass = refs
    img_ref[...] = jnp.zeros_like(img_ref)
    hits = jnp.zeros((8, IMG), F32)
    for j in range(4):
        cols = slice(j * IMG, (j + 1) * IMG)
        dots = (dots0, dots1)[j % 2]
        dots[...] = lax.dot_general(
            t_ref[...], x_ref[cols, :], (((1,), (1,)), ((), ())), preferred_element_type=F32
        )
        ids = (lax.broadcasted_iota(jnp.int32, (1, IMG), 1) + j * IMG).astype(F32)
        weight = weight_ref[j : j + 1, :]
        top = jnp.full((8, IMG), -VERY_HIGH, F32)
        for n in range(0, CAP, CHUNK):
            at = slice(n, n + CHUNK)
            target = column_ref[d * CAP + n : d * CAP + n + CHUNK, :]
            limit = wide(limit_ref[d * CAP + n : d * CAP + n + CHUNK, :], IMG)
            s = jnp.minimum(dots[at, :] * SCALE_LOG2, limit)
            s_ref[at, cols] = s
            top = jnp.maximum(top, fold(jnp.maximum, s))
            hits = hits + fold(jnp.add, jnp.where(wide(target, IMG) == ids, s * weight, 0.0))
            new = functools.reduce(jnp.maximum, tiles(s))
            if j:
                old = peak[at, :]
                new = jnp.maximum(new, old)
                mass[at, :] = mass[at, :] * jnp.exp2(old - new)
            peak[at, :] = new
        top = jnp.max(top, axis=0, keepdims=True)
        total = jnp.zeros((8, IMG), F32)
        for n in range(0, CAP, CHUNK):
            at = slice(n, n + CHUNK)
            s = s_ref[at, cols]
            total = total + fold(jnp.add, jnp.exp2(s - top))
            add = sum(jnp.exp2(p - peak[at, :]) for p in tiles(s))
            mass[at, :] = mass[at, :] + add if j else add
        img_ref[j : j + 1, :] = top + jnp.log2(jnp.sum(total, axis=0, keepdims=True))
    img_ref[4:5, :] = jnp.sum(hits, axis=0, keepdims=True)
    top = jnp.max(peak[...], axis=1, keepdims=True)
    total = jnp.sum(mass[...] * jnp.exp2(peak[...] - top), axis=1, keepdims=True)
    cap_ref[...] = jnp.zeros_like(cap_ref)
    cap_ref[d : d + 1, :] = row_of(top + jnp.log2(total))
    if others:
        img, cap = others[0::2], others[1::2]
        img_ref[0:4, :] = log_sum([img_ref[0:4, :]] + [o[0:4, :] for o in img])
        img_ref[4:5, :] = sum((o[4:5, :] for o in img), img_ref[4:5, :])
        cap_ref[...] = sum((o[...] for o in cap), cap_ref[...])


def scores(d, images, text, column, limit, weight, others):
    return call(
        functools.partial(scores_kernel, d, len(others) // 2),
        [((CAP, ROWS), F32), ((8, IMG), F32), ((8, CAP), F32)],
        (images, text, column, limit, weight, *others),
        scratch=[pltpu.VMEM((CAP, IMG), F32)] * 2 + [pltpu.VMEM((CAP, 128), F32)] * 2,
    )


def stats_kernel(
    share, scal_ref, img0, img1, img2, img3, cap0, cap1, cap2, cap3, mine_ref, r_ref, c_ref, a_ref, b_ref
):
    pick = lambda ref, order: jnp.concatenate([ref[o : o + 1, :] for o in order], axis=0)
    imgs, caps = (img0, img1, img2, img3), (cap0, cap1, cap2, cap3)
    r = log_sum([pick(ref, [j ^ q for j in range(4)]) for q, ref in enumerate(imgs)])
    r_ref[0:4, :] = r + 1.0
    r_ref[4:8, :] = jnp.zeros((4, IMG), F32)
    alive = mine_ref[0:4, :] >= 0.0
    c = log_sum([pick(ref, [(d + e) % 4 for d in range(4)]) for e, ref in enumerate(caps)])
    c = jnp.where(alive, c, 0.0)
    moved = jnp.where(alive, c - jnp.log2(scal_ref[0:1, 0:1]), 0.0)
    for d in range(4):
        c_ref[d * CAP : (d + 1) * CAP, :] = column_of(moved[d : d + 1, :])
    hits = sum(ref[4:5, :] for ref in imgs)
    a = (jnp.sum(r) * 0.5 - jnp.sum(hits)) * (LN2 / share)
    a = jnp.full((8, WIDTH), a, F32)
    high = a.astype(BF16).astype(F32)
    a_ref[0:8, :] = high
    a_ref[8:16, :] = a - high
    b_ref[...] = jnp.broadcast_to(jnp.sum(c) * scal_ref[1:2, :], (8, 128))


def statistics(share, scal, imgs, caps, mine):
    return call(
        functools.partial(stats_kernel, share),
        [((8, IMG), F32), ((4 * CAP, 128), F32), ((16, WIDTH), F32), ((8, 128), F32)],
        (scal, *imgs, *caps, mine),
    )


def split_weights(d, j, s_ref, r_ref, c_ref, column_ref, weight_ref, high_ref, low_ref):
    ids = (lax.broadcasted_iota(jnp.int32, (1, IMG), 1) + j * IMG).astype(F32)
    r = r_ref[j : j + 1, :]
    weight = weight_ref[j : j + 1, :]
    for n in range(0, CAP, CHUNK):
        rows = slice(d * CAP + n, d * CAP + n + CHUNK)
        s = s_ref[n : n + CHUNK, j * IMG : (j + 1) * IMG]
        w = jnp.exp2(s - r) + jnp.exp2(s - wide(c_ref[rows, :], IMG))
        w = w - jnp.where(wide(column_ref[rows, :], IMG) == ids, weight, 0.0)
        high = w.astype(BF16)
        high_ref[n : n + CHUNK, :] = high
        low_ref[n : n + CHUNK, :] = (w - high.astype(F32)).astype(BF16)


TERMS = [pltpu.VMEM((CAP, IMG), BF16)] * 4


def text_kernel(
    d, s_ref, x_ref, r_ref, c_ref, column_ref, weight_ref, o_ref, *terms
):
    acc = None
    for j in range(4):
        x = x_ref[j * IMG : (j + 1) * IMG, :]
        parts = terms[j % 2 * 2 : j % 2 * 2 + 2]
        split_weights(d, j, s_ref, r_ref, c_ref, column_ref, weight_ref, *parts)
        for part in parts:
            term = jnp.dot(part[...], x, preferred_element_type=F32)
            acc = term if acc is None else acc + term
    o_ref[...] = acc


def text_terms(d, s, images, r, c, column, weight):
    return call(
        functools.partial(text_kernel, d),
        [((CAP, WIDTH), F32)],
        (s, images, r, c, column, weight),
        scratch=TERMS,
    )[0]


def image_kernel(
    js, s0, s1, s2, s3, t0, t1, t2, t3, r_ref, c_ref, column_ref, weight_ref, *refs
):
    outs, terms = refs[: len(js)], refs[len(js) :]
    for j, y in zip(js, outs):
        acc = None
        for d, (s_ref, t) in enumerate(((s0, t0), (s1, t1), (s2, t2), (s3, t3))):
            parts = terms[d % 2 * 2 : d % 2 * 2 + 2]
            split_weights(d, j, s_ref, r_ref, c_ref, column_ref, weight_ref, *parts)
            for part in parts:
                term = lax.dot_general(
                    part[...], t[...], (((0,), (0,)), ((), ())), preferred_element_type=F32
                )
                acc = term if acc is None else acc + term
        y[...] = acc


def image_terms(js, s, texts, r, c, column, weight):
    return call(
        functools.partial(image_kernel, js),
        [((IMG, WIDTH), F32)] * len(js),
        (*s, *texts, r, c, column, weight),
        scratch=TERMS,
    )


def after(*values):
    return lax.optimization_barrier(values)


def pack(value):
    return (value * SEND_SCALE).astype(jnp.float16)


def unpack(value):
    return value.astype(F32) * (1.0 / SEND_SCALE)


def shards(images, captions, cap_target, cap_count):
    groups = lax.axis_size("dp")
    blocks = lax.axis_size("blk")
    me = lax.axis_index("blk")
    my_x, my_yc = lax.div(me, 4), lax.rem(me, 4)
    order = jnp.stack([lax.rem(my_x + d, XS) * 4 + my_yc for d in range(4)])
    base = jnp.stack([(my_x * 4 + (my_yc ^ q)) * IMG for q in range(4)])

    image1 = across(images, 1)
    image2 = across(images, 2)
    received = lax.all_to_all(captions, "dp", split_axis=0, concat_axis=0, tiled=True)
    weight, column, limit, mine, scal = setup(base, order, cap_count, cap_target)
    image2, weight, column, limit, mine, scal = after(image2, weight, column, limit, mine, scal)
    image3 = across(image2, 1)
    images = (images, image1, image2, image3)
    parts, column, limit, weight, mine, scal = join(images, column, limit, weight, mine, scal)
    texts = (received,) + tuple(along_x(received, -d) for d in (1, 2, 3))

    s, found = [None] * 4, []
    for d in (0, 1, 3, 2):
        s[d], img, cap = scores(d, parts, texts[d], column, limit, weight, found if d == 2 else [])
        found += [img, cap]
    imgs = (img,) + tuple(across(img, q) for q in (1, 2, 3))
    caps = (cap,) + tuple(along_x(cap, e) for e in (1, 2, 3))
    r, c, loss_x, loss_yc = statistics(IMG * blocks * groups, scal, imgs, caps, mine)
    loss_rows = loss_x.astype(jnp.float16)

    loss_yc = loss_yc + across(loss_yc, 2)
    (y3,) = image_terms((3,), s, texts, r, c, column, weight)
    a3 = across(pack(y3), 1)
    r, y3 = after(r, y3)
    sent = [None] * 4
    for d in (2, 1, 3):
        part = pack(text_terms(d, s[d], parts, r, c, column, weight))
        part = jnp.concatenate([part, loss_rows], axis=0)
        sent[d] = along_x(part, d)
        r, part = after(r, part)
        if d == 1:
            r, loss_yc = after(r, loss_yc)
            loss_yc = loss_yc + across(loss_yc, 1)
        if d == 3:
            r, loss_yc = after(r, loss_yc)
    (y2,) = image_terms((2,), s, texts, r, c, column, weight)
    packed = pack(y2 + unpack(a3))
    b = across(packed, 2)
    r, packed = after(r, packed)
    own = text_terms(0, s[0], parts, r, c, column, weight)
    r, own = after(r, own)
    y1, y0 = image_terms((1, 0), s, texts, r, c, column, weight)
    a1 = across(pack(y1), 1)
    y0, own, *sent = after(y0, own, *sent[1:])
    text_grad = pack(own + sum(unpack(v[:CAP]) for v in sent))
    loss = loss_yc + loss_x[0:8, :128] + loss_x[8:16, :128]
    loss = loss + sum(v[CAP : CAP + 8, :128].astype(F32) + v[CAP + 8 :, :128].astype(F32) for v in sent)
    high = lax.reduce_precision(loss, 5, 10)
    lane = lax.broadcasted_iota(jnp.int32, loss.shape, 1)
    loss_lanes = jnp.where(lane < HALF, high, loss - high).astype(jnp.float16)
    loss_lanes = jnp.broadcast_to(loss_lanes[0:1], (CAP, 2 * HALF))
    text_grad = jnp.concatenate([text_grad, loss_lanes], axis=1)
    text_grad, y0, packed = after(text_grad, y0, packed)
    text_grad = lax.all_to_all(text_grad, "dp", split_axis=0, concat_axis=0, tiled=True)
    image_grad = (y0 + unpack(a1) + unpack(b)) * LOGIT_SCALE
    text_grad, image_grad = after(text_grad, image_grad)
    grad_captions = unpack(text_grad[:, :WIDTH]) * LOGIT_SCALE
    loss_value = jnp.sum(text_grad[:, WIDTH:].astype(F32)) / (SLOT * HALF)
    return loss_value, image_grad, grad_captions


def solution(mesh):
    return jax.shard_map(
        shards,
        mesh=mesh,
        in_specs=(P(("dp", "blk"), None), P(("dp", "blk"), None), P("dp", None), P("dp", None)),
        out_specs=(P(), P(("dp", "blk"), None), P(("dp", "blk"), None)),
        check_vma=False,
    )
```

```python
import functools
import math

import jax
import jax.numpy as jnp
from jax import lax
from jax.experimental import pallas as pl
from jax.experimental.pallas import tpu as pltpu
from jax.sharding import PartitionSpec as P

LOGIT_SCALE = 50.0
SCALE_LOG2 = LOGIT_SCALE * math.log2(math.e)
LN2 = math.log(2.0)
SEND_SCALE = 16.0
VERY_LOW = -1e30
VERY_HIGH = 3e38
VMEM_BYTES = 20 * 1024 * 1024
F32 = jnp.float32
BF16 = jnp.bfloat16

XS, YS, CORES = 4, 2, 2
IMG = 512
CAP = 256
WIDTH = 768
ROWS = 4 * IMG
SLOT = 16
HALF = 64
CHUNK = 32


def call(kernel, out, args, smem=0, scratch=()):
    vmem = pl.BlockSpec(memory_space=pltpu.VMEM)
    scalars = [pl.BlockSpec(memory_space=pltpu.SMEM)] * smem
    return pl.pallas_call(
        kernel,
        out_shape=tuple(jax.ShapeDtypeStruct(*o) for o in out),
        in_specs=scalars + [vmem] * (len(args) - smem),
        out_specs=(vmem,) * len(out),
        scratch_shapes=list(scratch),
        compiler_params=pltpu.CompilerParams(vmem_limit_bytes=VMEM_BYTES),
        cost_estimate=pl.CostEstimate(flops=1 << 20, bytes_accessed=1 << 16, transcendentals=0),
    )(*args)


def move(value, there):
    spots = [(x, y, c) for x in range(XS) for y in range(YS) for c in range(CORES)]
    flat = lambda x, y, c: (x * YS + y) * CORES + c
    return lax.ppermute(value, "blk", [(flat(*s), flat(*there(*s))) for s in spots])


def along_x(value, shift):
    return move(value, lambda x, y, c: ((x + shift) % XS, y, c))


def across(value, q):
    return move(value, lambda x, y, c: (x, y ^ (q >> 1), c ^ (q & 1)))


def row_of(column, lanes=128):
    return jnp.broadcast_to(column, (column.shape[0], lanes)).T[0:1, :]


def column_of(row, lanes=128):
    return jnp.broadcast_to(row, (lanes, row.shape[1])).T


def wide(column, lanes):
    return jnp.concatenate([column] * (lanes // column.shape[1]), axis=1)


def log_sum(parts):
    peak = functools.reduce(jnp.maximum, parts)
    return peak + jnp.log2(sum(jnp.exp2(p - peak) for p in parts))


def setup_kernel(
    base_ref, order_ref, counts_ref, targets_in, weight_ref, column_ref, limit_ref, mine_ref, scal_ref, targets_ref
):
    blocks = targets_ref.shape[0]
    iota = lambda shape, dim: lax.broadcasted_iota(jnp.int32, shape, dim)
    counts = counts_ref[...].astype(F32)
    live = jnp.sum(counts, axis=1, keepdims=True)
    half_balance = 0.5 * IMG * blocks / live
    scal_ref[0:1, :] = jnp.broadcast_to(half_balance, (1, 128))
    scal_ref[1:2, :] = jnp.broadcast_to(LN2 * 0.5 / blocks / live, (1, 128))
    scal_ref[2:8, :] = jnp.zeros((6, 128), F32)
    slot = iota((CAP, CAP), 1) // SLOT
    spread = jnp.where(iota((CAP, CAP), 0) % SLOT == slot, 1.0, 0.0).astype(BF16)
    owned = jnp.where(iota((blocks, CAP), 1) // SLOT == iota((blocks, CAP), 0), counts, 0.0)
    filled = jnp.dot(owned.astype(BF16), spread, preferred_element_type=F32)
    for b in range(blocks):
        targets_ref[b : b + 1, :] = targets_in[0:1, b * CAP : (b + 1) * CAP].astype(F32)
    alive = (iota((blocks, CAP), 1) % SLOT).astype(F32) < filled
    targets_ref[...] = jnp.where(alive, targets_ref[...], -1.0)
    mine_ref[...] = jnp.zeros_like(mine_ref)
    for d in range(4):
        row = targets_ref[pl.ds(order_ref[d], 1), :]
        mine_ref[d : d + 1, :] = row
        place = jnp.full_like(row, -1.0)
        for j in range(4):
            at = row - base_ref[j].astype(F32)
            place = jnp.where((at >= 0.0) & (at < IMG), at + j * IMG, place)
        column_ref[d * CAP : (d + 1) * CAP, :] = column_of(place)
        limit_ref[d * CAP : (d + 1) * CAP, :] = column_of(jnp.where(row < 0.0, VERY_LOW, VERY_HIGH))
    weight_ref[...] = jnp.zeros_like(weight_ref)
    step = 256
    for i in range(ROWS // step):
        j, at = i * step // IMG, i * step % IMG
        ids = iota((step, 128), 0).astype(F32) + (base_ref[j] + at).astype(F32)

        def add(b, acc):
            row = targets_ref[pl.ds(b, 1), :]
            for h in range(CAP // 128):
                acc = acc + jnp.where(row[:, h * 128 : (h + 1) * 128] == ids, 1.0, 0.0)
            return acc

        hits = lax.fori_loop(0, blocks, add, jnp.zeros((step, 128), F32), unroll=2)
        count = jnp.sum(hits, axis=1, keepdims=True)
        weight_ref[j : j + 1, at : at + step] = row_of(0.5 / jnp.maximum(count, 1.0) + half_balance)


def setup(base, order, counts, targets):
    return call(
        setup_kernel,
        [((8, IMG), F32)] + [((4 * CAP, 128), F32)] * 2 + [((8, CAP), F32), ((8, 128), F32)],
        (base, order, counts, targets),
        smem=2,
        scratch=[pltpu.VMEM((targets.shape[1] // CAP, CAP), F32)],
    )


def join_kernel(x0, x1, x2, x3, *refs):
    ins, (x_ref, *outs) = refs[: len(refs) // 2], refs[len(refs) // 2 :]
    for j, x in enumerate((x0, x1, x2, x3)):
        x_ref[j * IMG : (j + 1) * IMG, :] = x[...]
    for i, o in zip(ins, outs):
        o[...] = i[...]


def join(images, *others):
    return call(
        join_kernel,
        [((ROWS, WIDTH), BF16)] + [(o.shape, o.dtype) for o in others],
        (*images, *others),
    )


def tiles(s):
    return [s[:, n : n + 128] for n in range(0, s.shape[1], 128)]


def fold(op, s):
    return functools.reduce(op, [s[n : n + 8, :] for n in range(0, s.shape[0], 8)])


def scores_kernel(d, n_others, *refs):
    (x_ref, t_ref, column_ref, limit_ref, weight_ref), refs = refs[:5], refs[5:]
    others, refs = refs[: 2 * n_others], refs[2 * n_others :]
    s_ref, img_ref, cap_ref, dots0, dots1, peak, mass = refs
    img_ref[...] = jnp.zeros_like(img_ref)
    hits = jnp.zeros((8, IMG), F32)
    for j in range(4):
        cols = slice(j * IMG, (j + 1) * IMG)
        dots = (dots0, dots1)[j % 2]
        dots[...] = lax.dot_general(
            t_ref[...], x_ref[cols, :], (((1,), (1,)), ((), ())), preferred_element_type=F32
        )
        ids = (lax.broadcasted_iota(jnp.int32, (1, IMG), 1) + j * IMG).astype(F32)
        weight = weight_ref[j : j + 1, :]
        top = jnp.full((8, IMG), -VERY_HIGH, F32)
        for n in range(0, CAP, CHUNK):
            at = slice(n, n + CHUNK)
            target = column_ref[d * CAP + n : d * CAP + n + CHUNK, :]
            limit = wide(limit_ref[d * CAP + n : d * CAP + n + CHUNK, :], IMG)
            s = jnp.minimum(dots[at, :] * SCALE_LOG2, limit)
            s_ref[at, cols] = s
            top = jnp.maximum(top, fold(jnp.maximum, s))
            hits = hits + fold(jnp.add, jnp.where(wide(target, IMG) == ids, s * weight, 0.0))
            new = functools.reduce(jnp.maximum, tiles(s))
            if j:
                old = peak[at, :]
                new = jnp.maximum(new, old)
                mass[at, :] = mass[at, :] * jnp.exp2(old - new)
            peak[at, :] = new
        top = jnp.max(top, axis=0, keepdims=True)
        total = jnp.zeros((8, IMG), F32)
        for n in range(0, CAP, CHUNK):
            at = slice(n, n + CHUNK)
            s = s_ref[at, cols]
            total = total + fold(jnp.add, jnp.exp2(s - top))
            add = sum(jnp.exp2(p - peak[at, :]) for p in tiles(s))
            mass[at, :] = mass[at, :] + add if j else add
        img_ref[j : j + 1, :] = top + jnp.log2(jnp.sum(total, axis=0, keepdims=True))
    img_ref[4:5, :] = jnp.sum(hits, axis=0, keepdims=True)
    top = jnp.max(peak[...], axis=1, keepdims=True)
    total = jnp.sum(mass[...] * jnp.exp2(peak[...] - top), axis=1, keepdims=True)
    cap_ref[...] = jnp.zeros_like(cap_ref)
    cap_ref[d : d + 1, :] = row_of(top + jnp.log2(total))
    if others:
        img, cap = others[0::2], others[1::2]
        img_ref[0:4, :] = log_sum([img_ref[0:4, :]] + [o[0:4, :] for o in img])
        img_ref[4:5, :] = sum((o[4:5, :] for o in img), img_ref[4:5, :])
        cap_ref[...] = sum((o[...] for o in cap), cap_ref[...])


def scores(d, images, text, column, limit, weight, others):
    return call(
        functools.partial(scores_kernel, d, len(others) // 2),
        [((CAP, ROWS), F32), ((8, IMG), F32), ((8, CAP), F32)],
        (images, text, column, limit, weight, *others),
        scratch=[pltpu.VMEM((CAP, IMG), F32)] * 2 + [pltpu.VMEM((CAP, 128), F32)] * 2,
    )


def stats_kernel(
    share, scal_ref, img0, img1, img2, img3, cap0, cap1, cap2, cap3, mine_ref, r_ref, c_ref, a_ref, b_ref
):
    pick = lambda ref, order: jnp.concatenate([ref[o : o + 1, :] for o in order], axis=0)
    imgs, caps = (img0, img1, img2, img3), (cap0, cap1, cap2, cap3)
    r = log_sum([pick(ref, [j ^ q for j in range(4)]) for q, ref in enumerate(imgs)])
    r_ref[0:4, :] = r + 1.0
    r_ref[4:8, :] = jnp.zeros((4, IMG), F32)
    alive = mine_ref[0:4, :] >= 0.0
    c = log_sum([pick(ref, [(d + e) % 4 for d in range(4)]) for e, ref in enumerate(caps)])
    c = jnp.where(alive, c, 0.0)
    moved = jnp.where(alive, c - jnp.log2(scal_ref[0:1, 0:1]), 0.0)
    for d in range(4):
        c_ref[d * CAP : (d + 1) * CAP, :] = column_of(moved[d : d + 1, :])
    hits = sum(ref[4:5, :] for ref in imgs)
    a = (jnp.sum(r) * 0.5 - jnp.sum(hits)) * (LN2 / share)
    a = jnp.full((8, WIDTH), a, F32)
    high = a.astype(BF16).astype(F32)
    a_ref[0:8, :] = high
    a_ref[8:16, :] = a - high
    b_ref[...] = jnp.broadcast_to(jnp.sum(c) * scal_ref[1:2, :], (8, 128))


def statistics(share, scal, imgs, caps, mine):
    return call(
        functools.partial(stats_kernel, share),
        [((8, IMG), F32), ((4 * CAP, 128), F32), ((16, WIDTH), F32), ((8, 128), F32)],
        (scal, *imgs, *caps, mine),
    )


def split_weights(d, j, s_ref, r_ref, c_ref, column_ref, weight_ref, high_ref, low_ref):
    ids = (lax.broadcasted_iota(jnp.int32, (1, IMG), 1) + j * IMG).astype(F32)
    r = r_ref[j : j + 1, :]
    weight = weight_ref[j : j + 1, :]
    for n in range(0, CAP, CHUNK):
        rows = slice(d * CAP + n, d * CAP + n + CHUNK)
        s = s_ref[n : n + CHUNK, j * IMG : (j + 1) * IMG]
        w = jnp.exp2(s - r) + jnp.exp2(s - wide(c_ref[rows, :], IMG))
        w = w - jnp.where(wide(column_ref[rows, :], IMG) == ids, weight, 0.0)
        high = w.astype(BF16)
        high_ref[n : n + CHUNK, :] = high
        low_ref[n : n + CHUNK, :] = (w - high.astype(F32)).astype(BF16)


TERMS = [pltpu.VMEM((CAP, IMG), BF16)] * 4


def text_kernel(
    d, s_ref, x_ref, r_ref, c_ref, column_ref, weight_ref, o_ref, *terms
):
    acc = None
    for j in range(4):
        x = x_ref[j * IMG : (j + 1) * IMG, :]
        parts = terms[j % 2 * 2 : j % 2 * 2 + 2]
        split_weights(d, j, s_ref, r_ref, c_ref, column_ref, weight_ref, *parts)
        for part in parts:
            term = jnp.dot(part[...], x, preferred_element_type=F32)
            acc = term if acc is None else acc + term
    o_ref[...] = acc


def text_terms(d, s, images, r, c, column, weight):
    return call(
        functools.partial(text_kernel, d),
        [((CAP, WIDTH), F32)],
        (s, images, r, c, column, weight),
        scratch=TERMS,
    )[0]


def image_kernel(
    js, s0, s1, s2, s3, t0, t1, t2, t3, r_ref, c_ref, column_ref, weight_ref, *refs
):
    outs, terms = refs[: len(js)], refs[len(js) :]
    for j, y in zip(js, outs):
        acc = None
        for d, (s_ref, t) in enumerate(((s0, t0), (s1, t1), (s2, t2), (s3, t3))):
            parts = terms[d % 2 * 2 : d % 2 * 2 + 2]
            split_weights(d, j, s_ref, r_ref, c_ref, column_ref, weight_ref, *parts)
            for part in parts:
                term = lax.dot_general(
                    part[...], t[...], (((0,), (0,)), ((), ())), preferred_element_type=F32
                )
                acc = term if acc is None else acc + term
        y[...] = acc


def image_terms(js, s, texts, r, c, column, weight):
    return call(
        functools.partial(image_kernel, js),
        [((IMG, WIDTH), F32)] * len(js),
        (*s, *texts, r, c, column, weight),
        scratch=TERMS,
    )


def after(*values):
    return lax.optimization_barrier(values)


def pack(value):
    return (value * SEND_SCALE).astype(jnp.float16)


def unpack(value):
    return value.astype(F32) * (1.0 / SEND_SCALE)


def shards(images, captions, cap_target, cap_count):
    groups = lax.axis_size("dp")
    blocks = lax.axis_size("blk")
    me = lax.axis_index("blk")
    my_x, my_yc = lax.div(me, 4), lax.rem(me, 4)
    order = jnp.stack([lax.rem(my_x + d, XS) * 4 + my_yc for d in range(4)])
    base = jnp.stack([(my_x * 4 + (my_yc ^ q)) * IMG for q in range(4)])

    image1 = across(images, 1)
    image2 = across(images, 2)
    received = lax.all_to_all(captions, "dp", split_axis=0, concat_axis=0, tiled=True)
    weight, column, limit, mine, scal = setup(base, order, cap_count, cap_target)
    image2, weight, column, limit, mine, scal = after(image2, weight, column, limit, mine, scal)
    image3 = across(image2, 1)
    images = (images, image1, image2, image3)
    parts, column, limit, weight, mine, scal = join(images, column, limit, weight, mine, scal)
    texts = (received,) + tuple(along_x(received, -d) for d in (1, 2, 3))

    s, found = [None] * 4, []
    for d in (0, 1, 3, 2):
        s[d], img, cap = scores(d, parts, texts[d], column, limit, weight, found if d == 2 else [])
        found += [img, cap]
    imgs = (img,) + tuple(across(img, q) for q in (1, 2, 3))
    caps = (cap,) + tuple(along_x(cap, e) for e in (1, 2, 3))
    r, c, loss_x, loss_yc = statistics(IMG * blocks * groups, scal, imgs, caps, mine)
    loss_rows = loss_x.astype(jnp.float16)

    loss_yc = loss_yc + across(loss_yc, 2)
    (y3,) = image_terms((3,), s, texts, r, c, column, weight)
    a3 = across(pack(y3), 1)
    r, y3 = after(r, y3)
    sent = [None] * 4
    for d in (2, 1, 3):
        part = pack(text_terms(d, s[d], parts, r, c, column, weight))
        part = jnp.concatenate([part, loss_rows], axis=0)
        sent[d] = along_x(part, d)
        r, part = after(r, part)
        if d == 1:
            r, loss_yc = after(r, loss_yc)
            loss_yc = loss_yc + across(loss_yc, 1)
    (y2,) = image_terms((2,), s, texts, r, c, column, weight)
    packed = pack(y2 + unpack(a3))
    b = across(packed, 2)
    r, packed = after(r, packed)
    own = text_terms(0, s[0], parts, r, c, column, weight)
    r, own = after(r, own)
    y1, y0 = image_terms((1, 0), s, texts, r, c, column, weight)
    a1 = jnp.concatenate([across(pack(y1[h]), 1) for h in (slice(0, IMG // 2), slice(IMG // 2, IMG))], axis=0)
    y0, own, *sent = after(y0, own, *sent[1:])
    text_grad = pack(own + sum(unpack(v[:CAP]) for v in sent))
    loss = loss_yc + loss_x[0:8, :128] + loss_x[8:16, :128]
    loss = loss + sum(v[CAP : CAP + 8, :128].astype(F32) + v[CAP + 8 :, :128].astype(F32) for v in sent)
    high = lax.reduce_precision(loss, 5, 10)
    lane = lax.broadcasted_iota(jnp.int32, loss.shape, 1)
    loss_lanes = jnp.where(lane < HALF, high, loss - high).astype(jnp.float16)
    loss_lanes = jnp.broadcast_to(loss_lanes[0:1], (CAP, 2 * HALF))
    text_grad = jnp.concatenate([text_grad, loss_lanes], axis=1)
    text_grad, y0, packed = after(text_grad, y0, packed)
    text_grad = lax.all_to_all(text_grad, "dp", split_axis=0, concat_axis=0, tiled=True)
    image_grad = (y0 + unpack(a1) + unpack(b)) * LOGIT_SCALE
    text_grad, image_grad = after(text_grad, image_grad)
    grad_captions = unpack(text_grad[:, :WIDTH]) * LOGIT_SCALE
    loss_value = jnp.sum(text_grad[:, WIDTH:].astype(F32)) / (SLOT * HALF)
    return loss_value, image_grad, grad_captions


def solution(mesh):
    return jax.shard_map(
        shards,
        mesh=mesh,
        in_specs=(P(("dp", "blk"), None), P(("dp", "blk"), None), P("dp", None), P("dp", None)),
        out_specs=(P(), P(("dp", "blk"), None), P(("dp", "blk"), None)),
        check_vma=False,
    )
```

```python
import functools
import math

import jax
import jax.numpy as jnp
from jax import lax
from jax.experimental import pallas as pl
from jax.experimental.pallas import tpu as pltpu
from jax.sharding import PartitionSpec as P

LOGIT_SCALE = 50.0
SCALE_LOG2 = LOGIT_SCALE * math.log2(math.e)
LN2 = math.log(2.0)
SEND_SCALE = 16.0
VERY_LOW = -1e30
VERY_HIGH = 3e38
VMEM_BYTES = 20 * 1024 * 1024
F32 = jnp.float32
BF16 = jnp.bfloat16

XS, YS, CORES = 4, 2, 2
IMG = 512
CAP = 256
WIDTH = 768
ROWS = 4 * IMG
SLOT = 16
HALF = 64
CHUNK = 32


def call(kernel, out, args, smem=0, scratch=()):
    vmem = pl.BlockSpec(memory_space=pltpu.VMEM)
    scalars = [pl.BlockSpec(memory_space=pltpu.SMEM)] * smem
    return pl.pallas_call(
        kernel,
        out_shape=tuple(jax.ShapeDtypeStruct(*o) for o in out),
        in_specs=scalars + [vmem] * (len(args) - smem),
        out_specs=(vmem,) * len(out),
        scratch_shapes=list(scratch),
        compiler_params=pltpu.CompilerParams(vmem_limit_bytes=VMEM_BYTES),
        cost_estimate=pl.CostEstimate(flops=1 << 20, bytes_accessed=1 << 16, transcendentals=0),
    )(*args)


def move(value, there):
    spots = [(x, y, c) for x in range(XS) for y in range(YS) for c in range(CORES)]
    flat = lambda x, y, c: (x * YS + y) * CORES + c
    return lax.ppermute(value, "blk", [(flat(*s), flat(*there(*s))) for s in spots])


def along_x(value, shift):
    return move(value, lambda x, y, c: ((x + shift) % XS, y, c))


def across(value, q):
    return move(value, lambda x, y, c: (x, y ^ (q >> 1), c ^ (q & 1)))


def row_of(column, lanes=128):
    return jnp.broadcast_to(column, (column.shape[0], lanes)).T[0:1, :]


def column_of(row, lanes=128):
    return jnp.broadcast_to(row, (lanes, row.shape[1])).T


def wide(column, lanes):
    return jnp.concatenate([column] * (lanes // column.shape[1]), axis=1)


def log_sum(parts):
    peak = functools.reduce(jnp.maximum, parts)
    return peak + jnp.log2(sum(jnp.exp2(p - peak) for p in parts))


def setup_kernel(
    base_ref, order_ref, counts_ref, targets_in, weight_ref, column_ref, limit_ref, mine_ref, scal_ref, targets_ref
):
    blocks = targets_ref.shape[0]
    iota = lambda shape, dim: lax.broadcasted_iota(jnp.int32, shape, dim)
    counts = counts_ref[...].astype(F32)
    live = jnp.sum(counts, axis=1, keepdims=True)
    half_balance = 0.5 * IMG * blocks / live
    scal_ref[0:1, :] = jnp.broadcast_to(half_balance, (1, 128))
    scal_ref[1:2, :] = jnp.broadcast_to(LN2 * 0.5 / blocks / live, (1, 128))
    scal_ref[2:8, :] = jnp.zeros((6, 128), F32)
    slot = iota((CAP, CAP), 1) // SLOT
    spread = jnp.where(iota((CAP, CAP), 0) % SLOT == slot, 1.0, 0.0).astype(BF16)
    owned = jnp.where(iota((blocks, CAP), 1) // SLOT == iota((blocks, CAP), 0), counts, 0.0)
    filled = jnp.dot(owned.astype(BF16), spread, preferred_element_type=F32)
    for b in range(blocks):
        targets_ref[b : b + 1, :] = targets_in[0:1, b * CAP : (b + 1) * CAP].astype(F32)
    alive = (iota((blocks, CAP), 1) % SLOT).astype(F32) < filled
    targets_ref[...] = jnp.where(alive, targets_ref[...], -1.0)
    mine_ref[...] = jnp.zeros_like(mine_ref)
    for d in range(4):
        row = targets_ref[pl.ds(order_ref[d], 1), :]
        mine_ref[d : d + 1, :] = row
        place = jnp.full_like(row, -1.0)
        for j in range(4):
            at = row - base_ref[j].astype(F32)
            place = jnp.where((at >= 0.0) & (at < IMG), at + j * IMG, place)
        column_ref[d * CAP : (d + 1) * CAP, :] = column_of(place)
        limit_ref[d * CAP : (d + 1) * CAP, :] = column_of(jnp.where(row < 0.0, VERY_LOW, VERY_HIGH))
    weight_ref[...] = jnp.zeros_like(weight_ref)
    step = 256
    for i in range(ROWS // step):
        j, at = i * step // IMG, i * step % IMG
        ids = iota((step, 128), 0).astype(F32) + (base_ref[j] + at).astype(F32)

        def add(b, acc):
            row = targets_ref[pl.ds(b, 1), :]
            for h in range(CAP // 128):
                acc = acc + jnp.where(row[:, h * 128 : (h + 1) * 128] == ids, 1.0, 0.0)
            return acc

        hits = lax.fori_loop(0, blocks, add, jnp.zeros((step, 128), F32), unroll=2)
        count = jnp.sum(hits, axis=1, keepdims=True)
        weight_ref[j : j + 1, at : at + step] = row_of(0.5 / jnp.maximum(count, 1.0) + half_balance)


def setup(base, order, counts, targets):
    return call(
        setup_kernel,
        [((8, IMG), F32)] + [((4 * CAP, 128), F32)] * 2 + [((8, CAP), F32), ((8, 128), F32)],
        (base, order, counts, targets),
        smem=2,
        scratch=[pltpu.VMEM((targets.shape[1] // CAP, CAP), F32)],
    )


def join_kernel(x0, x1, x2, x3, *refs):
    ins, (x_ref, *outs) = refs[: len(refs) // 2], refs[len(refs) // 2 :]
    for j, x in enumerate((x0, x1, x2, x3)):
        x_ref[j * IMG : (j + 1) * IMG, :] = x[...]
    for i, o in zip(ins, outs):
        o[...] = i[...]


def join(images, *others):
    return call(
        join_kernel,
        [((ROWS, WIDTH), BF16)] + [(o.shape, o.dtype) for o in others],
        (*images, *others),
    )


def tiles(s):
    return [s[:, n : n + 128] for n in range(0, s.shape[1], 128)]


def fold(op, s):
    return functools.reduce(op, [s[n : n + 8, :] for n in range(0, s.shape[0], 8)])


def scores_kernel(d, n_others, *refs):
    (x_ref, t_ref, column_ref, limit_ref, weight_ref), refs = refs[:5], refs[5:]
    others, refs = refs[: 2 * n_others], refs[2 * n_others :]
    s_ref, img_ref, cap_ref, dots0, dots1, peak, mass = refs
    img_ref[...] = jnp.zeros_like(img_ref)
    hits = jnp.zeros((8, IMG), F32)
    for j in range(4):
        cols = slice(j * IMG, (j + 1) * IMG)
        dots = (dots0, dots1)[j % 2]
        dots[...] = lax.dot_general(
            t_ref[...], x_ref[cols, :], (((1,), (1,)), ((), ())), preferred_element_type=F32
        )
        ids = (lax.broadcasted_iota(jnp.int32, (1, IMG), 1) + j * IMG).astype(F32)
        weight = weight_ref[j : j + 1, :]
        top = jnp.full((8, IMG), -VERY_HIGH, F32)
        for n in range(0, CAP, CHUNK):
            at = slice(n, n + CHUNK)
            target = column_ref[d * CAP + n : d * CAP + n + CHUNK, :]
            limit = wide(limit_ref[d * CAP + n : d * CAP + n + CHUNK, :], IMG)
            s = jnp.minimum(dots[at, :] * SCALE_LOG2, limit)
            s_ref[at, cols] = s
            top = jnp.maximum(top, fold(jnp.maximum, s))
            hits = hits + fold(jnp.add, jnp.where(wide(target, IMG) == ids, s * weight, 0.0))
            new = functools.reduce(jnp.maximum, tiles(s))
            if j:
                old = peak[at, :]
                new = jnp.maximum(new, old)
                mass[at, :] = mass[at, :] * jnp.exp2(old - new)
            peak[at, :] = new
        top = jnp.max(top, axis=0, keepdims=True)
        total = jnp.zeros((8, IMG), F32)
        for n in range(0, CAP, CHUNK):
            at = slice(n, n + CHUNK)
            s = s_ref[at, cols]
            total = total + fold(jnp.add, jnp.exp2(s - top))
            add = sum(jnp.exp2(p - peak[at, :]) for p in tiles(s))
            mass[at, :] = mass[at, :] + add if j else add
        img_ref[j : j + 1, :] = top + jnp.log2(jnp.sum(total, axis=0, keepdims=True))
    img_ref[4:5, :] = jnp.sum(hits, axis=0, keepdims=True)
    top = jnp.max(peak[...], axis=1, keepdims=True)
    total = jnp.sum(mass[...] * jnp.exp2(peak[...] - top), axis=1, keepdims=True)
    cap_ref[...] = jnp.zeros_like(cap_ref)
    cap_ref[d : d + 1, :] = row_of(top + jnp.log2(total))
    if others:
        img, cap = others[0::2], others[1::2]
        img_ref[0:4, :] = log_sum([img_ref[0:4, :]] + [o[0:4, :] for o in img])
        img_ref[4:5, :] = sum((o[4:5, :] for o in img), img_ref[4:5, :])
        cap_ref[...] = sum((o[...] for o in cap), cap_ref[...])


def scores(d, images, text, column, limit, weight, others):
    return call(
        functools.partial(scores_kernel, d, len(others) // 2),
        [((CAP, ROWS), F32), ((8, IMG), F32), ((8, CAP), F32)],
        (images, text, column, limit, weight, *others),
        scratch=[pltpu.VMEM((CAP, IMG), F32)] * 2 + [pltpu.VMEM((CAP, 128), F32)] * 2,
    )


def stats_kernel(
    share, scal_ref, img0, img1, img2, img3, cap0, cap1, cap2, cap3, mine_ref, r_ref, c_ref, a_ref, b_ref
):
    pick = lambda ref, order: jnp.concatenate([ref[o : o + 1, :] for o in order], axis=0)
    imgs, caps = (img0, img1, img2, img3), (cap0, cap1, cap2, cap3)
    r = log_sum([pick(ref, [j ^ q for j in range(4)]) for q, ref in enumerate(imgs)])
    r_ref[0:4, :] = r + 1.0
    r_ref[4:8, :] = jnp.zeros((4, IMG), F32)
    alive = mine_ref[0:4, :] >= 0.0
    c = log_sum([pick(ref, [(d + e) % 4 for d in range(4)]) for e, ref in enumerate(caps)])
    c = jnp.where(alive, c, 0.0)
    moved = jnp.where(alive, c - jnp.log2(scal_ref[0:1, 0:1]), 0.0)
    for d in range(4):
        c_ref[d * CAP : (d + 1) * CAP, :] = column_of(moved[d : d + 1, :])
    hits = sum(ref[4:5, :] for ref in imgs)
    a = (jnp.sum(r) * 0.5 - jnp.sum(hits)) * (LN2 / share)
    a = jnp.full((8, WIDTH), a, F32)
    high = a.astype(BF16).astype(F32)
    a_ref[0:8, :] = high
    a_ref[8:16, :] = a - high
    b_ref[...] = jnp.broadcast_to(jnp.sum(c) * scal_ref[1:2, :], (8, 128))


def statistics(share, scal, imgs, caps, mine):
    return call(
        functools.partial(stats_kernel, share),
        [((8, IMG), F32), ((4 * CAP, 128), F32), ((16, WIDTH), F32), ((8, 128), F32)],
        (scal, *imgs, *caps, mine),
    )


def split_weights(d, j, s_ref, r_ref, c_ref, column_ref, weight_ref, high_ref, low_ref):
    ids = (lax.broadcasted_iota(jnp.int32, (1, IMG), 1) + j * IMG).astype(F32)
    r = r_ref[j : j + 1, :]
    weight = weight_ref[j : j + 1, :]
    for n in range(0, CAP, CHUNK):
        rows = slice(d * CAP + n, d * CAP + n + CHUNK)
        s = s_ref[n : n + CHUNK, j * IMG : (j + 1) * IMG]
        w = jnp.exp2(s - r) + jnp.exp2(s - wide(c_ref[rows, :], IMG))
        w = w - jnp.where(wide(column_ref[rows, :], IMG) == ids, weight, 0.0)
        high = w.astype(BF16)
        high_ref[n : n + CHUNK, :] = high
        low_ref[n : n + CHUNK, :] = (w - high.astype(F32)).astype(BF16)


TERMS = [pltpu.VMEM((CAP, IMG), BF16)] * 4


def text_kernel(
    d, s_ref, x_ref, r_ref, c_ref, column_ref, weight_ref, o_ref, *terms
):
    acc = None
    for j in range(4):
        x = x_ref[j * IMG : (j + 1) * IMG, :]
        parts = terms[j % 2 * 2 : j % 2 * 2 + 2]
        split_weights(d, j, s_ref, r_ref, c_ref, column_ref, weight_ref, *parts)
        for part in parts:
            term = jnp.dot(part[...], x, preferred_element_type=F32)
            acc = term if acc is None else acc + term
    o_ref[...] = acc


def text_terms(d, s, images, r, c, column, weight):
    return call(
        functools.partial(text_kernel, d),
        [((CAP, WIDTH), F32)],
        (s, images, r, c, column, weight),
        scratch=TERMS,
    )[0]


def image_kernel(
    js, s0, s1, s2, s3, t0, t1, t2, t3, r_ref, c_ref, column_ref, weight_ref, *refs
):
    outs, terms = refs[: len(js)], refs[len(js) :]
    for j, y in zip(js, outs):
        acc = None
        for d, (s_ref, t) in enumerate(((s0, t0), (s1, t1), (s2, t2), (s3, t3))):
            parts = terms[d % 2 * 2 : d % 2 * 2 + 2]
            split_weights(d, j, s_ref, r_ref, c_ref, column_ref, weight_ref, *parts)
            for part in parts:
                term = lax.dot_general(
                    part[...], t[...], (((0,), (0,)), ((), ())), preferred_element_type=F32
                )
                acc = term if acc is None else acc + term
        y[...] = acc


def image_terms(js, s, texts, r, c, column, weight):
    return call(
        functools.partial(image_kernel, js),
        [((IMG, WIDTH), F32)] * len(js),
        (*s, *texts, r, c, column, weight),
        scratch=TERMS,
    )


def after(*values):
    return lax.optimization_barrier(values)


def pack(value):
    return (value * SEND_SCALE).astype(jnp.float16)


def unpack(value):
    return value.astype(F32) * (1.0 / SEND_SCALE)


def shards(images, captions, cap_target, cap_count):
    groups = lax.axis_size("dp")
    blocks = lax.axis_size("blk")
    me = lax.axis_index("blk")
    my_x, my_yc = lax.div(me, 4), lax.rem(me, 4)
    order = jnp.stack([lax.rem(my_x + d, XS) * 4 + my_yc for d in range(4)])
    base = jnp.stack([(my_x * 4 + (my_yc ^ q)) * IMG for q in range(4)])

    image1 = across(images, 1)
    image2 = across(images, 2)
    received = lax.all_to_all(captions, "dp", split_axis=0, concat_axis=0, tiled=True)
    weight, column, limit, mine, scal = setup(base, order, cap_count, cap_target)
    image2, weight, column, limit, mine, scal = after(image2, weight, column, limit, mine, scal)
    image3 = across(image2, 1)
    images = (images, image1, image2, image3)
    parts, column, limit, weight, mine, scal = join(images, column, limit, weight, mine, scal)
    texts = (received,) + tuple(along_x(received, -d) for d in (1, 2, 3))

    s, found = [None] * 4, []
    for d in (0, 1, 3, 2):
        s[d], img, cap = scores(d, parts, texts[d], column, limit, weight, found if d == 2 else [])
        found += [img, cap]
    imgs = (img,) + tuple(across(img, q) for q in (1, 2, 3))
    caps = (cap,) + tuple(along_x(cap, e) for e in (1, 2, 3))
    r, c, loss_x, loss_yc = statistics(IMG * blocks * groups, scal, imgs, caps, mine)
    loss_rows = loss_x.astype(jnp.float16)

    loss_yc = loss_yc + across(loss_yc, 2)
    (y3,) = image_terms((3,), s, texts, r, c, column, weight)
    a3 = across(pack(y3), 1)
    r, y3 = after(r, y3)
    sent = [None] * 4
    for d in (2, 1, 3):
        part = pack(text_terms(d, s[d], parts, r, c, column, weight))
        part = jnp.concatenate([part, loss_rows], axis=0)
        sent[d] = along_x(part, d)
        r, part = after(r, part)
        if d == 1:
            r, loss_yc = after(r, loss_yc)
            loss_yc = loss_yc + across(loss_yc, 1)
    (y2,) = image_terms((2,), s, texts, r, c, column, weight)
    packed = pack(y2 + unpack(a3))
    b = across(packed, 2)
    r, packed = after(r, packed)
    own = text_terms(0, s[0], parts, r, c, column, weight)
    r, own = after(r, own)
    y1, y0 = image_terms((1, 0), s, texts, r, c, column, weight)
    a1 = across(pack(y1), 1)
    y0, own, *sent = after(y0, own, *sent[1:])
    text_grad = pack(own + sum(unpack(v[:CAP]) for v in sent))
    loss = loss_yc + loss_x[0:8, :128] + loss_x[8:16, :128]
    loss = loss + sum(v[CAP : CAP + 8, :128].astype(F32) + v[CAP + 8 :, :128].astype(F32) for v in sent)
    high = lax.reduce_precision(loss, 5, 10)
    lane = lax.broadcasted_iota(jnp.int32, loss.shape, 1)
    loss_lanes = jnp.where(lane < HALF, high, loss - high).astype(jnp.float16)
    loss_lanes = jnp.broadcast_to(loss_lanes[0:1], (CAP, 2 * HALF))
    text_grad = jnp.concatenate([text_grad, loss_lanes], axis=1)
    text_grad, y0, packed = after(text_grad, y0, packed)
    text_grad = lax.all_to_all(text_grad, "dp", split_axis=0, concat_axis=0, tiled=True)
    image_grad = (y0 + unpack(a1) + unpack(b)) * LOGIT_SCALE
    text_grad, image_grad = after(text_grad, image_grad)
    grad_captions = unpack(text_grad[:, :WIDTH]) * LOGIT_SCALE
    loss_value = jnp.sum(text_grad[:, WIDTH:].astype(F32)) / (SLOT * HALF)
    return loss_value, image_grad, grad_captions


def solution(mesh):
    return jax.shard_map(
        shards,
        mesh=mesh,
        in_specs=(P(("dp", "blk"), None), P(("dp", "blk"), None), P("dp", None), P("dp", None)),
        out_specs=(P(), P(("dp", "blk"), None), P(("dp", "blk"), None)),
        check_vma=False,
    )
```
